128 devices in a mesh: lon: 8 (over z, core), lat: 16 (over x, y).
Axes of the slice: x: 4, y: 4, z: 4, core: 2. Of those that a mesh axis runs over, the one named last changes fastest.
Arguments:
- obs_rows: bfloat16 [2048, 128, 256], P(('lon', 'lat')), may hold values from -3 to 3
- innovations: bfloat16 [2048, 128], P(('lon', 'lat')), may hold values from -12 to 12
- obs_home: int32 [2048], replicated, may hold values from 0 to 2047, as said below
- obs_lists: int32 [16, 32, 48], P('lon', 'lat'), may hold values from -1 to 2047, as said below
- loc_weights: float32 [16, 32, 48], P('lon', 'lat'), may hold values from 0.05 to 1
- state_mean: float32 [32, 64, 512], P('lon', 'lat'), may hold values from -6 to 6
- state_perturb: bfloat16 [32, 64, 512, 256], P('lon', 'lat'), may hold values from -6 to 6
- interp_ids: int32 [32, 64, 4], P('lon', 'lat'), may hold values from 0 to 511, as said below
- interp_wts: float32 [32, 64, 4], P('lon', 'lat'), as said below
Outputs:
- analysis: bfloat16 [32, 64, 512, 256], P('lon', 'lat')
The draws below stay inside these ranges and needn't reach their ends.
Inputs may be any that keep to these rules, and one draw needn't show every extreme that they name: `obs_lists`: each entry is a block id or -1 (padding); in every list the ids come first, 12 or more of them, and ids may repeat. Block b lies in row obs_home[b] of obs_rows. Over the lists of one device's 2 x 2 analysis points, at most 2 entries (repeats counted) name blocks whose rows lie on one device; in every draw some device is named 2 times by the lists of every device. `obs_home`: A permutation of the rows of obs_rows. `interp_ids`: four distinct analysis points, each on the tile's device or at most one analysis point beyond that device's block of points along either dimension. `interp_wts`: Positive; the four weights of a tile sum to one.
All inputs are finite; a program needn't handle non-finite values. Where the reference program divides by a largest or mean magnitude, that divisor is 1e-20 or more.
Results may differ from the reference program's by a relative error of at most 0.0042.
Values may be sent and summed in bfloat16 or wider, within the bound.
No kernel may reach another device: no remote copies, remote signals or barrier semaphores. Data moves between devices by JAX's collectives and lax.ppermute only.
A program may use at most 192 MiB of HBM per device.

```python
import math
import jax
import jax.numpy as jnp
from jax import lax

K = 256
OBS = 128
LIST = 48
APX = 2
APY = 2
TX = 4
TY = 4
CELLS = 512
OB_DEV = 16
ITERS = 5
CAP = 2
NBLK = 2048
NAPX = 16
NAPY = 32
NTX = 32
NTY = 64
N_LON = 8
N_LAT = 16
DEVICES = 128


def draw_obs_lists(key, part):
    key = jax.random.fold_in(key, 11)
    key_forced, key_devices = jax.random.split(key)
    entries = APX * APY * LIST
    slots = DEVICES * CAP
    forced = jax.random.randint(key_forced, (), 0, DEVICES)

    def device_lists(device_key):
        key_slot, key_count, key_entry, key_local = jax.random.split(device_key, 4)
        slot = jnp.arange(slots, dtype=jnp.int32)
        shuffled = jax.random.permutation(key_slot, slots).astype(jnp.int32)
        slot_key = jnp.where(slot % DEVICES == forced, slot // DEVICES - slots, shuffled)
        sequence = slot[jnp.argsort(slot_key, stable=True)][:entries]
        counts = jax.random.randint(key_count, (APX * APY,), LIST // 4, LIST + 1)
        position = jnp.arange(entries, dtype=jnp.int32)
        live = position % LIST < counts[position // LIST]
        entry_key = jnp.where(live, 0, entries) + jax.random.permutation(key_entry, entries).astype(jnp.int32)
        entry_order = jnp.argsort(entry_key, stable=True)
        rank_of = jnp.zeros((entries,), jnp.int32).at[entry_order].set(position)
        owner = sequence[rank_of] % DEVICES
        local = jax.random.randint(key_local, (entries,), 0, OB_DEV)
        return jnp.where(live, owner * OB_DEV + local, -1).astype(jnp.int32)
    lists = jax.vmap(device_lists)(jax.random.split(key_devices, DEVICES))
    lists = lists.reshape(N_LON, N_LAT, APX, APY, LIST).transpose(0, 2, 1, 3, 4)
    return lists.reshape(NAPX, NAPY, LIST)


def draw_obs_home(key, part):
    key = jax.random.fold_in(key, 12)
    shuffles = jax.vmap(lambda device_key: jax.random.permutation(device_key, OB_DEV))(jax.random.split(key, DEVICES))
    base = jnp.arange(DEVICES, dtype=jnp.int32)[:, None] * OB_DEV
    return (base + shuffles.astype(jnp.int32)).reshape(-1)


def draw_interp_ids(key, part):
    key = jax.random.fold_in(key, 13)
    key_row, key_col = jax.random.split(key)
    tile_row = jnp.arange(NTX, dtype=jnp.int32)[:, None]
    tile_col = jnp.arange(NTY, dtype=jnp.int32)[None, :]
    offset_row = jax.random.randint(key_row, (NTX, NTY), 0, APX + 1)
    offset_col = jax.random.randint(key_col, (NTX, NTY), 0, APY + 1)
    first_row = jnp.clip(tile_row // TX * APX - 1 + offset_row, 0, NAPX - 2)
    first_col = jnp.clip(tile_col // TY * APY - 1 + offset_col, 0, NAPY - 2)
    corner = first_row * NAPY + first_col
    return jnp.stack([corner, corner + NAPY, corner + 1, corner + NAPY + 1], axis=-1).astype(jnp.int32)


def draw_interp_wts(key, part):
    key = jax.random.fold_in(key, 14)
    key_row, key_col = jax.random.split(key)
    along_row = jax.random.uniform(key_row, (NTX, NTY), jnp.float32, 0.05, 0.95)
    along_col = jax.random.uniform(key_col, (NTX, NTY), jnp.float32, 0.05, 0.95)
    return jnp.stack([(1.0 - along_row) * (1.0 - along_col), along_row * (1.0 - along_col), (1.0 - along_row) * along_col, along_row * along_col], axis=-1)


def levels(key, extent, cuts, low, top_value):
    loudness = 1.0
    for axis_at, shards_of in cuts:
        heights = jax.random.uniform(jax.random.fold_in(jax.random.fold_in(key, 6), axis_at), (shards_of,), jnp.float32, low / len(cuts), top_value / len(cuts))
        loudness = loudness * jnp.repeat(jnp.exp(heights), extent[axis_at] // shards_of).reshape((-1,) + (1,) * (len(extent) - 1 - axis_at))
    return loudness


def scatter_about(own_key, shape, width, limit, cuts=(), kind=jnp.bfloat16):
    values = jax.random.normal(own_key, shape, jnp.float32) * width
    if len(cuts) > 0:
        values = levels(own_key, shape, cuts, -0.22, 0.18) * values
    return jnp.clip(values, min=-limit, max=limit).astype(kind)


def setup_inputs(seed: int = 0) -> dict:
    streams_of = jax.random.split(jax.random.key(seed), 10)
    obs_rows = scatter_about(streams_of[0], (NBLK, OBS, K), 0.5, 3.0, ((0, 128),))
    innovations = scatter_about(streams_of[1], (NBLK, OBS), 2.0, 12.0, ((0, 128),))
    obs_home = draw_obs_home(jax.random.fold_in(streams_of[9], 71), 0)
    obs_lists = draw_obs_lists(jax.random.fold_in(streams_of[9], 71), 0)
    loc_weights = jnp.clip(jnp.exp(math.log(1.0) - 2.9957323 * jax.random.uniform(streams_of[4], (NAPX, NAPY, LIST), jnp.float32) ** levels(streams_of[4], (NAPX, NAPY, LIST), ((0, 8), (1, 16)), -0.2, 0.2)), 0.05, 1.0)
    state_mean = scatter_about(streams_of[5], (NTX, NTY, CELLS), 1.0, 6.0, ((0, 8), (1, 16)), jnp.float32)
    state_perturb = scatter_about(streams_of[6], (NTX, NTY, CELLS, K), 1.0, 6.0, ((0, 8), (1, 16)))
    interp_ids = draw_interp_ids(jax.random.fold_in(streams_of[9], 71), 0)
    interp_wts = draw_interp_wts(jax.random.fold_in(streams_of[9], 71), 0)
    return dict(obs_rows=obs_rows, innovations=innovations, obs_home=obs_home, obs_lists=obs_lists, loc_weights=loc_weights, state_mean=state_mean, state_perturb=state_perturb, interp_ids=interp_ids, interp_wts=interp_wts)


highest = lax.Precision.HIGHEST

def inverse_root(covariance, drive):
    members = covariance.shape[0]
    identity = jnp.eye(members, dtype=jnp.float32)
    system = identity + covariance / (members - 1)
    bound = jnp.max(lax.optimization_barrier(jnp.sum(jnp.abs(system), axis=1)))
    upper = system / bound
    lower = identity
    for sweep in range(ITERS):
        factor = 1.5 * identity - 0.5 * jnp.dot(lower, upper, precision=highest)
        upper = jnp.dot(upper, factor, precision=highest)
        lower = jnp.dot(factor, lower, precision=highest)
    root = lower / jnp.sqrt(bound)
    shift = jnp.dot(root, jnp.dot(root, drive, precision=highest), precision=highest)
    return (root + shift[:, None]).astype(jnp.bfloat16)

def point_weights(blocks, increments, weight_live):
    members = blocks.shape[2]
    wide = blocks.astype(jnp.float32)
    grams = jnp.einsum('lok,lom->lkm', wide, wide, precision=highest)
    covariance = jnp.einsum('l,lkm->km', weight_live, grams, precision=highest)
    project = jnp.einsum('lok,lo->lk', wide, increments.astype(jnp.float32), precision=highest)
    drive = jnp.dot(weight_live, project, precision=highest) / (members - 1)
    return inverse_root(covariance, drive)

def reference(obs_rows, innovations, obs_home, obs_lists, loc_weights, state_mean, state_perturb, interp_ids, interp_wts):
    point_rows, point_cols, list_len = obs_lists.shape
    members = obs_rows.shape[2]
    entry_ids = obs_lists.reshape(-1, list_len)
    live = entry_ids >= 0
    block_rows = obs_home[jnp.maximum(entry_ids, 0)].astype(jnp.int32)
    weight_live = jnp.where(live, loc_weights.reshape(-1, list_len), jnp.float32(0.0))

    def one_point(packed):
        rows_here, weight_here = packed
        return point_weights(obs_rows[rows_here], innovations[rows_here], weight_here)
    weights = lax.map(one_point, (block_rows, weight_live))
    tile_rows, tile_cols, cells = state_mean.shape

    def one_tile(packed):
        ids_here, wts_here, mean_here, pert_here = packed
        chosen = weights[ids_here].astype(jnp.float32)
        mixed = jnp.einsum('j,jkm->km', wts_here, chosen, precision=highest).astype(jnp.bfloat16)
        moved = jnp.dot(pert_here, mixed, preferred_element_type=jnp.float32)
        return (mean_here[:, None] + moved).astype(jnp.bfloat16)
    result = lax.map(one_tile, (interp_ids.reshape(-1, 4), interp_wts.reshape(-1, 4), state_mean.reshape(-1, cells), state_perturb.reshape(-1, cells, members)))
    return result.reshape(tile_rows, tile_cols, cells, members)
```

```python
import functools

import jax
import jax.numpy as jnp
from jax import lax
from jax.experimental import pallas as pl
from jax.experimental.pallas import tpu as pltpu
from jax.sharding import PartitionSpec as P

ITERS = 5
FAST = 4
bf16 = jnp.bfloat16
f32 = jnp.float32
highest = lax.Precision.HIGHEST


def split(x):
    hi = x.astype(bf16)
    return hi, (x - hi.astype(f32)).astype(bf16)


def mm(a, b):
    left = jnp.concatenate([a[0], a[0], a[1]], axis=1)
    right = jnp.concatenate([b[0], b[1], b[0]], axis=0)
    return jnp.dot(left, right, preferred_element_type=f32)


def gram_kernel(points, ranks, slots, wts, y_ref, proj_ref, o_ref, acc_ref):
    dest = pl.program_id(0)
    half = y_ref.shape[2] // 2
    row = lax.broadcasted_iota(jnp.int32, (half, half), 0)
    col = lax.broadcasted_iota(jnp.int32, (half, half), 1)
    for p in range(points):
        at = p * ranks
        ys = [y_ref[slots[dest, at + k]] for k in range(FAST)]
        yw = [(ys[k].astype(f32) * wts[dest, at + k]).astype(bf16) for k in range(FAST)]
        acc_ref[p] = lax.dot_general(
            jnp.concatenate(yw, axis=0),
            jnp.concatenate(ys, axis=0),
            (((0,), (0,)), ((), ())),
            preferred_element_type=f32,
        )
        count = slots[dest, points * ranks + p]

        @pl.loop(FAST, jnp.maximum(count, FAST))
        def _(k):
            y = y_ref[slots[dest, at + k]]
            w = (y.astype(f32) * wts[dest, at + k]).astype(bf16)
            acc_ref[p] += lax.dot_general(
                w, y, (((0,), (0,)), ((), ())), preferred_element_type=f32
            )

        drive = lax.fori_loop(
            0,
            count,
            lambda k, total: total + wts[dest, at + k] * proj_ref[slots[dest, at + k]],
            jnp.zeros(proj_ref.shape[1:], f32),
        )
        lower_right = acc_ref[p, half:, half:]
        o_ref[0, p, :half] = acc_ref[p, half:, :half].astype(bf16)
        o_ref[0, p, half : 2 * half] = jnp.where(
            row >= col, acc_ref[p, :half, :half], lower_right
        ).astype(bf16)
        diagonal = jnp.sum(jnp.where(row == col, lower_right, 0.0), axis=0, keepdims=True)
        diag_hi, diag_lo = split(diagonal)
        drive_hi, drive_lo = split(drive)
        tail = jnp.concatenate(
            [
                v.astype(f32)
                for v in (diag_hi, diag_lo, drive_hi, drive_lo)
            ]
            + [jnp.zeros((10, half), f32)],
            axis=0,
        )
        o_ref[0, p, 2 * half :] = tail.astype(bf16)


def root_kernel(parts_ref, o_ref):
    sources, points, _, half = parts_ref.shape
    members = 2 * half
    row = lax.broadcasted_iota(jnp.int32, (half, half), 0)
    col = lax.broadcasted_iota(jnp.int32, (half, half), 1)
    eye = (
        lax.broadcasted_iota(jnp.int32, (members, members), 0)
        == lax.broadcasted_iota(jnp.int32, (members, members), 1)
    ).astype(f32)
    for p in range(points):
        total = parts_ref[0, p].astype(f32)
        for s in range(1, sources):
            total = total + parts_ref[s, p].astype(f32)
        corner = total[:half]
        both = total[half:members]
        turned = both.T
        diagonal = total[members : members + 1] + total[members + 1 : members + 2]
        upper_left = jnp.where(row >= col, both, turned)
        lower_right = jnp.where(
            row == col, jnp.broadcast_to(diagonal, (half, half)), jnp.where(row < col, both, turned)
        )
        cov = jnp.concatenate(
            [
                jnp.concatenate([upper_left, corner.T], axis=1),
                jnp.concatenate([corner, lower_right], axis=1),
            ],
            axis=0,
        )
        scale = 1.0 / (members - 1)
        drive = (
            jnp.concatenate(
                [
                    total[members + 2 + h : members + 3 + h] + total[members + 4 + h : members + 5 + h]
                    for h in range(2)
                ],
                axis=1,
            )
            * scale
        )
        system = eye + cov * scale
        bound = jnp.max(jnp.sum(jnp.abs(system), axis=0, keepdims=True), axis=1, keepdims=True)
        upper = system * (1.0 / bound)
        factor = 1.5 * eye - 0.5 * upper
        factor_s = split(factor)
        lower, lower_s = factor, factor_s
        upper_s = split(mm(split(upper), factor_s))
        for sweep in range(1, ITERS):
            factor_s = split(1.5 * eye - 0.5 * mm(lower_s, upper_s))
            if sweep < ITERS - 1:
                upper_s = split(mm(upper_s, factor_s))
            lower = mm(factor_s, lower_s)
            lower_s = split(lower)
        root = lower * lax.rsqrt(bound)
        root_s = split(root)
        once = mm(split(jnp.broadcast_to(drive, (16, members))), root_s)[:1]
        shift = jnp.sum(root * once, axis=1, keepdims=True)
        o_ref[p] = (root + shift).astype(bf16)


def state_kernel(places, mixing, mean_ref, pert_ref, w_ref, o_ref):
    tile = pl.program_id(0)
    total = mixing[tile, 0] * w_ref[places[tile, 0]].astype(f32)
    for j in range(1, 4):
        total = total + mixing[tile, j] * w_ref[places[tile, j]].astype(f32)
    moved = jnp.dot(pert_ref[0], total.astype(bf16), preferred_element_type=f32)
    mean = jnp.broadcast_to(mean_ref[0], (8, mean_ref.shape[2])).T[:, :1]
    o_ref[0] = (mean + moved).astype(bf16)


def with_halo(cells, sides, width):
    for axis, dim in sides:
        count = lax.axis_size(axis)
        ends = count - 1
        head = lax.slice_in_dim(cells, 0, width, axis=dim)
        tail = lax.slice_in_dim(cells, cells.shape[dim] - width, cells.shape[dim], axis=dim)
        cells = jnp.concatenate(
            [
                lax.ppermute(tail, axis, [(i, (i + 1) % count) for i in range(ends)]),
                cells,
                lax.ppermute(head, axis, [((i + 1) % count, i) for i in range(ends)]),
            ],
            axis=dim,
        )
    return cells


def local(
    obs_rows,
    innovations,
    obs_home,
    obs_lists,
    loc_weights,
    state_mean,
    state_perturb,
    interp_ids,
    interp_wts,
):
    lon_count = lax.axis_size("lon")
    lat_count = lax.axis_size("lat")
    held, obs_count, members = obs_rows.shape
    half = members // 2
    point_rows, point_cols, list_len = obs_lists.shape
    points = point_rows * point_cols
    ranks = 2 * lon_count

    column_rows = lax.all_gather(obs_rows, "lon", tiled=True)
    project = jnp.einsum("lok,lo->lk", obs_rows, innovations, preferred_element_type=f32)
    column_proj = lax.all_gather(project, "lon", tiled=True).reshape(lon_count * held, 2, half)

    ids = obs_lists.reshape(points, list_len)
    live = ids >= 0
    home = jnp.take(obs_home, jnp.maximum(ids, 0))
    column = jnp.where(live, home // held % lat_count, lat_count)
    slot = home // (held * lat_count) * held + home % held
    mask = column[None] == jnp.arange(lat_count, dtype=jnp.int32)[:, None, None]
    rank = jnp.cumsum(mask.astype(jnp.int32), axis=2) - 1
    chosen = mask[..., None] & (rank[..., None] == jnp.arange(ranks, dtype=jnp.int32))
    slots_f = jnp.sum(jnp.where(chosen, slot.astype(f32)[None, :, :, None], 0.0), axis=2)
    wts_f = jnp.sum(
        jnp.where(chosen, loc_weights.reshape(1, points, list_len, 1), 0.0), axis=2
    )
    counts = jnp.sum(mask.astype(f32), axis=2)
    asked = jnp.concatenate(
        [
            slots_f.reshape(lat_count, points * ranks),
            counts,
            wts_f.reshape(lat_count, points * ranks),
        ],
        axis=1,
    )
    asked = lax.all_to_all(asked, "lat", 0, 0, tiled=True)
    cut = points * ranks + points
    slots = asked[:, :cut].astype(jnp.int32)
    wts = asked[:, cut:]

    smem = pl.BlockSpec(memory_space=pltpu.SMEM)
    vmem = pl.BlockSpec(memory_space=pltpu.VMEM)
    rows = members + 16
    partial = pl.pallas_call(
        functools.partial(gram_kernel, points, ranks),
        grid=(lat_count,),
        out_shape=jax.ShapeDtypeStruct((lat_count, points, rows, half), bf16),
        in_specs=[smem, smem, vmem, vmem],
        out_specs=pl.BlockSpec((1, points, rows, half), lambda i: (i, 0, 0, 0)),
        scratch_shapes=[pltpu.VMEM((points, members, members), f32)],
        compiler_params=pltpu.CompilerParams(vmem_limit_bytes=40 << 20),
        cost_estimate=pl.CostEstimate(
            flops=2 * 64 * 512 * 256 * 256, bytes_accessed=13 << 20, transcendentals=0
        ),
        name="gram",
    )(slots, wts, column_rows, column_proj)
    parts = lax.all_to_all(partial, "lat", 0, 0, tiled=True)

    group = 2
    weights = pl.pallas_call(
        root_kernel,
        grid=(points // group,),
        out_shape=jax.ShapeDtypeStruct((points, members, members), bf16),
        in_specs=[pl.BlockSpec((lat_count, group, rows, half), lambda i: (0, i, 0, 0))],
        out_specs=pl.BlockSpec((group, members, members), lambda i: (i, 0, 0)),
        compiler_params=pltpu.CompilerParams(vmem_limit_bytes=40 << 20),
        cost_estimate=pl.CostEstimate(
            flops=4 * 36 * 2 * 256**3, bytes_accessed=5 << 20, transcendentals=0
        ),
        name="root",
    )(parts).reshape(point_rows, point_cols, members, members)

    widened = with_halo(weights, (("lat", 1), ("lon", 0)), 1)
    halo_rows = point_rows + 2
    halo_cols = point_cols + 2
    grid_cols = point_cols * lat_count
    tile_rows, tile_cols, cells = state_mean.shape
    tiles = tile_rows * tile_cols
    target_ids = interp_ids.reshape(tiles, 4)
    local_row = target_ids // grid_cols - (lax.axis_index("lon") * point_rows - 1)
    local_col = target_ids % grid_cols - (lax.axis_index("lat") * point_cols - 1)
    places = local_row * halo_cols + local_col
    result = pl.pallas_call(
        state_kernel,
        grid=(tiles,),
        out_shape=jax.ShapeDtypeStruct((tiles, cells, members), bf16),
        in_specs=[
            smem,
            smem,
            pl.BlockSpec((1, 1, cells), lambda i: (i, 0, 0)),
            pl.BlockSpec((1, cells, members), lambda i: (i, 0, 0)),
            vmem,
        ],
        out_specs=pl.BlockSpec((1, cells, members), lambda i: (i, 0, 0)),
        compiler_params=pltpu.CompilerParams(vmem_limit_bytes=40 << 20),
        cost_estimate=pl.CostEstimate(
            flops=2 * 16 * 512 * 256 * 256, bytes_accessed=11 << 20, transcendentals=0
        ),
        name="state",
    )(
        places,
        interp_wts.reshape(tiles, 4),
        state_mean.reshape(tiles, 1, cells),
        state_perturb.reshape(tiles, cells, members),
        widened.reshape(halo_rows * halo_cols, members, members),
    )
    return result.reshape(tile_rows, tile_cols, cells, members)


def solution(mesh):
    return jax.shard_map(
        local,
        mesh=mesh,
        in_specs=(
            P(("lon", "lat"), None, None),
            P(("lon", "lat"), None),
            P(),
            P("lon", "lat", None),
            P("lon", "lat", None),
            P("lon", "lat", None),
            P("lon", "lat", None, None),
            P("lon", "lat", None),
            P("lon", "lat", None),
        ),
        out_specs=P("lon", "lat", None, None),
        check_vma=False,
    )
```

```python
import functools

import jax
import jax.numpy as jnp
from jax import lax
from jax.experimental import pallas as pl
from jax.experimental.pallas import tpu as pltpu
from jax.sharding import PartitionSpec as P

ITERS = 5
FAST = 4
TAIL = 16
SIDE = 4
bf16 = jnp.bfloat16
f32 = jnp.float32
highest = lax.Precision.HIGHEST


def split(x):
    hi = x.astype(bf16)
    return hi, (x - hi.astype(f32)).astype(bf16)


def mm(a, b):
    left = jnp.concatenate([a[0], a[0], a[1]], axis=1)
    right = jnp.concatenate([b[0], b[1], b[0]], axis=0)
    return jnp.dot(left, right, preferred_element_type=f32)


def places_of(half):
    row = lax.broadcasted_iota(jnp.int32, (half, half), 0)
    col = lax.broadcasted_iota(jnp.int32, (half, half), 1)
    return row, col


def pack(matrix, vector_rows):
    half = matrix.shape[0] // 2
    row, col = places_of(half)
    lower_right = matrix[half:, half:]
    both = jnp.where(row >= col, matrix[:half, :half], lower_right)
    diagonal = jnp.sum(jnp.where(row == col, lower_right, 0.0), axis=0, keepdims=True)
    hi = diagonal.astype(bf16).astype(f32)
    tail = jnp.concatenate(
        [hi, diagonal - hi, vector_rows, jnp.zeros((TAIL - 6, half), f32)], axis=0
    )
    return matrix[half:, :half].astype(bf16), both.astype(bf16), tail.astype(bf16)


def unpack(total):
    half = total.shape[1]
    members = 2 * half
    row, col = places_of(half)
    corner = total[:half]
    both = total[half:members]
    turned = both.T
    diagonal = total[members : members + 1] + total[members + 1 : members + 2]
    upper_left = jnp.where(row >= col, both, turned)
    lower_right = jnp.where(
        row == col, jnp.broadcast_to(diagonal, (half, half)), jnp.where(row < col, both, turned)
    )
    matrix = jnp.concatenate(
        [
            jnp.concatenate([upper_left, corner.T], axis=1),
            jnp.concatenate([corner, lower_right], axis=1),
        ],
        axis=0,
    )
    vector = jnp.concatenate(
        [
            total[members + 2 + h : members + 3 + h] + total[members + 4 + h : members + 5 + h]
            for h in range(2)
        ],
        axis=1,
    )
    return matrix, vector


def vector_rows(vector, half):
    hi = vector.astype(bf16).astype(f32)
    lo = vector - hi
    return jnp.concatenate([hi[:, :half], hi[:, half:], lo[:, :half], lo[:, half:]], axis=0)


def gram_kernel(points, ranks, order, slots, wts, y_ref, drive_ref, a_ref, b_ref, acc_ref):
    step = pl.program_id(0)
    half = y_ref.shape[2] // 2
    units = [(order[0, step], p, a_ref) for p in range(0, points, 2)]
    units += [(order[1, step], p, b_ref) for p in range(1, points, 2)]
    most = jnp.int32(0)
    for u, (dest, p, _) in enumerate(units):
        at = p * ranks
        ys = [y_ref[slots[dest, at + k]] for k in range(FAST)]
        yw = [(ys[k].astype(f32) * wts[dest, at + k]).astype(bf16) for k in range(FAST)]
        acc_ref[u] = lax.dot_general(
            jnp.concatenate(yw, axis=0),
            jnp.concatenate(ys, axis=0),
            (((0,), (0,)), ((), ())),
            preferred_element_type=f32,
        )
        most = jnp.maximum(most, slots[dest, points * ranks + p])

    @pl.when(most > FAST)
    def _():
        for u, (dest, p, _) in enumerate(units):
            at = p * ranks

            @pl.loop(FAST, jnp.maximum(slots[dest, points * ranks + p], FAST))
            def _(k):
                y = y_ref[slots[dest, at + k]]
                w = (y.astype(f32) * wts[dest, at + k]).astype(bf16)
                acc_ref[u] += lax.dot_general(
                    w, y, (((0,), (0,)), ((), ())), preferred_element_type=f32
                )

    for u, (dest, p, o_ref) in enumerate(units):
        corner, both, tail = pack(acc_ref[u], drive_ref[dest, p])
        o_ref[0, p // 2, :half] = corner
        o_ref[0, p // 2, half : 2 * half] = both
        o_ref[0, p // 2, 2 * half :] = tail


def root_kernel(firsts, *refs):
    o_ref = refs[-1]
    parts = [r.at[0] for r in refs[:firsts]] + list(refs[firsts:-1])
    points, rows, half = o_ref.shape
    members = 2 * half
    eye = (
        lax.broadcasted_iota(jnp.int32, (members, members), 0)
        == lax.broadcasted_iota(jnp.int32, (members, members), 1)
    ).astype(f32)
    scale = 1.0 / (members - 1)
    for p in range(points):
        total = parts[0][p].astype(f32)
        for part in parts[1:]:
            total = total + part[p].astype(f32)
        cov, drive = unpack(total)
        drive = drive * scale
        system = eye + cov * scale
        bound = jnp.max(jnp.sum(jnp.abs(system), axis=0, keepdims=True), axis=1, keepdims=True)
        upper = system * (1.0 / bound)
        lower = 1.5 * eye - 0.5 * upper
        lower_s = split(lower)
        upper_s = split(mm(split(upper), lower_s))
        for sweep in range(1, ITERS):
            factor_s = split(1.5 * eye - 0.5 * mm(lower_s, upper_s))
            if sweep < ITERS - 1:
                upper_s = split(mm(upper_s, factor_s))
            lower = mm(factor_s, lower_s)
            lower_s = split(lower)
        root = lower * lax.rsqrt(bound)
        root_s = split(root)
        once = mm(split(jnp.broadcast_to(drive, (16, members))), root_s)
        shift = mm(split(once), root_s)[:1]
        corner, both, tail = pack(root, vector_rows(shift, half))
        o_ref[p, :half] = corner
        o_ref[p, half:members] = both
        o_ref[p, members:] = tail


def state_kernel(places, mixing, mean_ref, pert_ref, w_ref, o_ref):
    step = pl.program_id(0)
    count, cells, members = o_ref.shape
    for t in range(count):
        tile = step * count + t
        total = mixing[tile, 0] * w_ref[places[tile, 0]].astype(f32)
        for j in range(1, 4):
            total = total + mixing[tile, j] * w_ref[places[tile, j]].astype(f32)
        root, shift = unpack(total)
        shift = jnp.broadcast_to(shift, (8, members)).T[:, :1]
        moved = jnp.dot(pert_ref[t], (root + shift).astype(bf16), preferred_element_type=f32)
        mean = jnp.broadcast_to(mean_ref[t], (8, cells)).T[:, :1]
        o_ref[t] = (mean + moved).astype(bf16)


def column_of(rows):
    size = lax.axis_size("lon")
    up = [(i, (i + 2) % size) for i in range(size)]
    down = [(i, (i - 2) % size) for i in range(size)]
    cut = rows.shape[0] // 2

    def send(x, pairs):
        return lax.ppermute(x, "lon", pairs)

    def swap(x):
        return lax.ppermute(x, "lon", [(i, i ^ 1) for i in range(size)])

    below = send(rows, up)
    above = send(rows, down)
    far_a = send(below[:cut], up)
    far_b = send(above[cut:], down)
    mine = [rows, above, far_a, far_b, below]
    return jnp.concatenate(mine + [swap(x) for x in mine], axis=0)


def turn(along, k):
    pairs = []
    for x in range(SIDE):
        for y in range(SIDE):
            if along == "y":
                pairs.append((x * SIDE + y, x * SIDE + (y + k) % SIDE))
            else:
                pairs.append((x * SIDE + y, (x + k) % SIDE * SIDE + y))
    return pairs


def local(
    obs_rows,
    innovations,
    obs_home,
    obs_lists,
    loc_weights,
    state_mean,
    state_perturb,
    interp_ids,
    interp_wts,
):
    lon_count = lax.axis_size("lon")
    lat_count = lax.axis_size("lat")
    lon = lax.axis_index("lon")
    lat = lax.axis_index("lat")
    held, obs_count, members = obs_rows.shape
    half = members // 2
    point_rows, point_cols, list_len = obs_lists.shape
    points = point_rows * point_cols
    ranks = 2 * lon_count
    column_blocks = lon_count * held

    column_rows = column_of(obs_rows)
    project = jnp.einsum("lok,lo->lk", obs_rows, innovations, preferred_element_type=f32)
    column_proj = lax.all_gather(project, "lon", tiled=True)

    ids = obs_lists.reshape(points, list_len)
    live = ids >= 0
    home = jnp.take(obs_home, jnp.maximum(ids, 0))
    column = jnp.where(live, home // held % lat_count, lat_count)
    slot = home // (held * lat_count) * held + home % held
    mask = column[None] == jnp.arange(lat_count, dtype=jnp.int32)[:, None, None]
    rank = jnp.cumsum(mask.astype(jnp.int32), axis=2) - 1
    chosen = mask[..., None] & (rank[..., None] == jnp.arange(ranks, dtype=jnp.int32))
    slots_f = jnp.sum(jnp.where(chosen, slot.astype(f32)[None, :, :, None], 0.0), axis=2)
    wts_f = jnp.sum(
        jnp.where(chosen, loc_weights.reshape(1, points, list_len, 1), 0.0), axis=2
    )
    counts = jnp.sum(mask.astype(f32), axis=2)
    asked = jnp.concatenate(
        [
            slots_f.reshape(lat_count, points * ranks),
            counts,
            wts_f.reshape(lat_count, points * ranks),
        ],
        axis=1,
    )
    asked = lax.all_to_all(asked, "lat", 0, 0, tiled=True)
    cut = points * ranks + points
    wts = asked[:, cut:]
    named = asked[:, : points * ranks].astype(jnp.int32)
    from_lon = named // held
    apart = (from_lon // 2 - lon // 2) % (lon_count // 2) + (lon_count // 2) * (
        (from_lon + lon) % 2
    )
    slots = jnp.concatenate(
        [apart * held + named % held, asked[:, points * ranks : cut].astype(jnp.int32)], axis=1
    )

    spread = jnp.sum(
        jnp.where(
            named.reshape(lat_count * points, ranks, 1)
            == jnp.arange(column_blocks, dtype=jnp.int32),
            wts.reshape(lat_count * points, ranks, 1),
            0.0,
        ),
        axis=1,
    )
    drive = jnp.dot(spread, column_proj, precision=highest)
    drive_hi = drive.astype(bf16).astype(f32)
    drive_rows = jnp.concatenate(
        [v.reshape(lat_count, points, 2, half) for v in (drive_hi, drive - drive_hi)], axis=2
    )

    smem = pl.BlockSpec(memory_space=pltpu.SMEM)
    vmem = pl.BlockSpec(memory_space=pltpu.VMEM)
    rows = members + TAIL
    each = points // 2
    x, y = lat // SIDE, lat % SIDE
    others = jnp.arange(SIDE, dtype=jnp.int32)

    def gram(k):
        order = jnp.stack(
            [
                (x + others) % SIDE * SIDE + (y + k) % SIDE,
                (x + k) % SIDE * SIDE + (y + others) % SIDE,
            ]
        )
        shape = jax.ShapeDtypeStruct((SIDE, each, rows, half), bf16)
        block = pl.BlockSpec((1, each, rows, half), lambda i: (i, 0, 0, 0))
        return pl.pallas_call(
            functools.partial(gram_kernel, points, ranks),
            grid=(SIDE,),
            out_shape=(shape, shape),
            in_specs=[smem, smem, smem, vmem, vmem],
            out_specs=(block, block),
            scratch_shapes=[pltpu.VMEM((points, members, members), f32)],
            compiler_params=pltpu.CompilerParams(vmem_limit_bytes=24 << 20),
            cost_estimate=pl.CostEstimate(
                flops=2 * 16 * 512 * 256 * 256, bytes_accessed=10 << 20, transcendentals=0
            ),
            name="gram",
        )(order, slots, wts, column_rows, drive_rows)

    first = {0: [None, None]}
    kept = {}
    for k in (2, 1, 3):
        to_y, to_x = gram(k)
        first[k] = [
            lax.ppermute(to_y, "lat", turn("y", k)),
            lax.ppermute(to_x, "lat", turn("x", k)),
        ]
    first[0] = list(gram(0))

    def second(side, along):
        got = []
        for k in (2, 1, 3):
            total = first[0][side][k].astype(f32)
            for j in (1, 3, 2):
                total = total + first[j][side][k].astype(f32)
            got.append(lax.ppermute(total.astype(bf16), "lat", turn(along, k)))
        return got

    seconds = [second(0, "x"), second(1, "y")]

    def root(side):
        firsts = [first[j][side] for j in (0, 1, 3, 2)]
        one = pl.BlockSpec((1, each, rows, half), lambda i: (0, 0, 0, 0))
        whole = pl.BlockSpec((each, rows, half), lambda i: (0, 0, 0))
        return pl.pallas_call(
            functools.partial(root_kernel, len(firsts)),
            grid=(1,),
            out_shape=jax.ShapeDtypeStruct((each, rows, half), bf16),
            in_specs=[one] * len(firsts) + [whole] * len(seconds[side]),
            out_specs=whole,
            compiler_params=pltpu.CompilerParams(vmem_limit_bytes=24 << 20),
            cost_estimate=pl.CostEstimate(
                flops=2 * 36 * 2 * 256**3, bytes_accessed=2 << 20, transcendentals=0
            ),
            name="root",
        )(*firsts, *seconds[side])

    col_a = root(0)
    right = lax.ppermute(col_a, "lat", [(i + 1, i) for i in range(lat_count - 1)])
    col_b = root(1)
    left = lax.ppermute(col_b, "lat", [(i, i + 1) for i in range(lat_count - 1)])
    cols = [left, col_a, col_b, right]
    below = lax.ppermute(
        jnp.stack([c[0] for c in cols]), "lon", [(i + 1, i) for i in range(lon_count - 1)]
    )
    above = lax.ppermute(
        jnp.stack([c[1] for c in cols]), "lon", [(i, i + 1) for i in range(lon_count - 1)]
    )
    held_w = jnp.concatenate(cols + [above, below], axis=0)

    grid_cols = point_cols * lat_count
    tile_rows, tile_cols, cells = state_mean.shape
    tiles = tile_rows * tile_cols
    target_ids = interp_ids.reshape(tiles, 4)
    local_row = target_ids // grid_cols - lon * point_rows
    local_col = target_ids % grid_cols - lat * point_cols + 1
    places = jnp.where(
        local_row < 0,
        2 * 4 + local_col,
        jnp.where(local_row >= point_rows, 3 * 4 + local_col, local_col * 2 + local_row),
    )
    per = 2
    result = pl.pallas_call(
        state_kernel,
        grid=(tiles // per,),
        out_shape=jax.ShapeDtypeStruct((tiles, cells, members), bf16),
        in_specs=[
            smem,
            smem,
            pl.BlockSpec((per, 1, cells), lambda i: (i, 0, 0)),
            pl.BlockSpec((per, cells, members), lambda i: (i, 0, 0)),
            vmem,
        ],
        out_specs=pl.BlockSpec((per, cells, members), lambda i: (i, 0, 0)),
        compiler_params=pltpu.CompilerParams(vmem_limit_bytes=24 << 20),
        cost_estimate=pl.CostEstimate(
            flops=2 * 16 * 512 * 256 * 256, bytes_accessed=11 << 20, transcendentals=0
        ),
        name="state",
    )(
        places,
        interp_wts.reshape(tiles, 4),
        state_mean.reshape(tiles, 1, cells),
        state_perturb.reshape(tiles, cells, members),
        held_w,
    )
    return result.reshape(tile_rows, tile_cols, cells, members)


def solution(mesh):
    return jax.shard_map(
        local,
        mesh=mesh,
        in_specs=(
            P(("lon", "lat"), None, None),
            P(("lon", "lat"), None),
            P(),
            P("lon", "lat", None),
            P("lon", "lat", None),
            P("lon", "lat", None),
            P("lon", "lat", None, None),
            P("lon", "lat", None),
            P("lon", "lat", None),
        ),
        out_specs=P("lon", "lat", None, None),
        check_vma=False,
    )
```

```python
import functools

import jax
import jax.numpy as jnp
from jax import lax
from jax.experimental import pallas as pl
from jax.experimental.pallas import tpu as pltpu
from jax.sharding import PartitionSpec as P

ITERS = 5
FAST = 4
TAIL = 16
SIDE = 4
GRANT = 12 << 20
bf16 = jnp.bfloat16
f32 = jnp.float32
highest = lax.Precision.HIGHEST


def product(a, b):
    rest = jnp.dot(a[1].astype(bf16), b[1].astype(bf16), preferred_element_type=f32)
    return a[0] * b[0], a[0] * b[1] + b[0] * a[1] + rest


def step_factor(a):
    return 1.5 - 0.5 * a[0], -0.5 * a[1]


def row_times(vector, a):
    hi = vector.astype(bf16).astype(f32)
    rows = jnp.concatenate([hi, vector - hi, jnp.zeros((14, vector.shape[1]), f32)], axis=0)
    got = jnp.dot(rows.astype(bf16), a[1].astype(bf16), preferred_element_type=f32)
    return a[0] * vector + jnp.sum(got[:2], axis=0, keepdims=True)


def places_of(half):
    row = lax.broadcasted_iota(jnp.int32, (half, half), 0)
    col = lax.broadcasted_iota(jnp.int32, (half, half), 1)
    return row, col


def pack(matrix, vector_rows):
    half = matrix.shape[0] // 2
    row, col = places_of(half)
    lower_right = matrix[half:, half:]
    both = jnp.where(row >= col, matrix[:half, :half], lower_right)
    diagonal = jnp.sum(jnp.where(row == col, lower_right, 0.0), axis=0, keepdims=True)
    hi = diagonal.astype(bf16).astype(f32)
    tail = jnp.concatenate(
        [hi, diagonal - hi, vector_rows, jnp.zeros((TAIL - 6, half), f32)], axis=0
    )
    return matrix[half:, :half].astype(bf16), both.astype(bf16), tail.astype(bf16)


def unpack(total):
    half = total.shape[1]
    members = 2 * half
    row, col = places_of(half)
    corner = total[:half]
    both = total[half:members]
    turned = both.T
    diagonal = total[members : members + 1] + total[members + 1 : members + 2]
    upper_left = jnp.where(row >= col, both, turned)
    lower_right = jnp.where(
        row == col, jnp.broadcast_to(diagonal, (half, half)), jnp.where(row < col, both, turned)
    )
    matrix = jnp.concatenate(
        [
            jnp.concatenate([upper_left, corner.T], axis=1),
            jnp.concatenate([corner, lower_right], axis=1),
        ],
        axis=0,
    )
    vector = jnp.concatenate(
        [
            total[members + 2 + h : members + 3 + h] + total[members + 4 + h : members + 5 + h]
            for h in range(2)
        ],
        axis=1,
    )
    return matrix, vector


def vector_rows(vector, half):
    hi = vector.astype(bf16).astype(f32)
    lo = vector - hi
    return jnp.concatenate([hi[:, :half], hi[:, half:], lo[:, :half], lo[:, half:]], axis=0)


def gram_kernel(points, ranks, order, slots, wts, drive_ref, *refs):
    pieces = refs[:-4]
    o_ref, acc_ref, y_ref, sem = refs[-4:]
    dest = order[pl.program_id(0)]
    half = y_ref.shape[2] // 2

    @pl.when(pl.program_id(0) == 0)
    def _():
        copies = []
        at = 0
        for i, piece in enumerate(pieces):
            copies.append(
                pltpu.make_async_copy(piece, y_ref.at[pl.ds(at, piece.shape[0])], sem.at[i])
            )
            copies[-1].start()
            at += piece.shape[0]
        for copy in copies:
            copy.wait()

    most = jnp.int32(0)
    for p in range(points):
        at = p * ranks
        ys = [y_ref[slots[dest, at + k]] for k in range(FAST)]
        yw = [(ys[k].astype(f32) * wts[dest, at + k]).astype(bf16) for k in range(FAST)]
        acc_ref[p] = lax.dot_general(
            jnp.concatenate(yw, axis=0),
            jnp.concatenate(ys, axis=0),
            (((0,), (0,)), ((), ())),
            preferred_element_type=f32,
        )
        most = jnp.maximum(most, slots[dest, points * ranks + p])

    @pl.when(most > FAST)
    def _():
        for p in range(points):
            at = p * ranks

            @pl.loop(FAST, jnp.maximum(slots[dest, points * ranks + p], FAST))
            def _(k):
                y = y_ref[slots[dest, at + k]]
                w = (y.astype(f32) * wts[dest, at + k]).astype(bf16)
                acc_ref[p] += lax.dot_general(
                    w, y, (((0,), (0,)), ((), ())), preferred_element_type=f32
                )

    for p in range(points):
        corner, both, tail = pack(acc_ref[p], drive_ref[dest, p])
        o_ref[0, p, :half] = corner
        o_ref[0, p, half : 2 * half] = both
        o_ref[0, p, 2 * half :] = tail


def root_kernel(*refs):
    parts, outs = refs[:-2], refs[-2:]
    points, rows, half = parts[0].shape
    members = 2 * half
    here = range(points)
    eye = (
        lax.broadcasted_iota(jnp.int32, (members, members), 0)
        == lax.broadcasted_iota(jnp.int32, (members, members), 1)
    ).astype(f32)
    scale = 1.0 / (members - 1)
    drives, bounds, uppers, lowers = [], [], [], []
    for p in here:
        total = parts[0][p].astype(f32)
        for part in parts[1:]:
            total = total + part[p].astype(f32)
        cov, drive = unpack(total)
        drives.append(drive * scale)
        system = eye + cov * scale
        bound = jnp.max(
            jnp.sum(jnp.abs(system), axis=0, keepdims=True), axis=1, keepdims=True
        )
        trace = jnp.sum(
            jnp.sum(system * eye, axis=0, keepdims=True), axis=1, keepdims=True
        )
        level = trace * (1.0 / members)
        inverse = 1.0 / bound
        bounds.append(bound)
        uppers.append((level * inverse, (system - level * eye) * inverse))
    lowers = [step_factor(uppers[p]) for p in here]
    uppers = [product(uppers[p], lowers[p]) for p in here]
    for sweep in range(1, ITERS):
        factors = [step_factor(product(lowers[p], uppers[p])) for p in here]
        if sweep < ITERS - 1:
            uppers = [product(uppers[p], factors[p]) for p in here]
        lowers = [product(factors[p], lowers[p]) for p in here]
    for p in here:
        norm = lax.rsqrt(bounds[p])
        root = (lowers[p][0] * norm, lowers[p][1] * norm)
        shift = row_times(row_times(drives[p], root), root)
        corner, both, tail = pack(root[1] + root[0] * eye, vector_rows(shift, half))
        o_ref, row = outs[p % 2], p // 2
        o_ref[row, :half] = corner
        o_ref[row, half:members] = both
        o_ref[row, members:] = tail


def state_kernel(places, mixing, mean_ref, pert_ref, w_ref, o_ref):
    step = pl.program_id(0)
    count, cells, members = o_ref.shape
    ones = jnp.ones((TAIL, members), bf16)
    for t in range(count):
        tile = step * count + t
        total = mixing[tile, 0] * w_ref[places[tile, 0]].astype(f32)
        for j in range(1, 4):
            total = total + mixing[tile, j] * w_ref[places[tile, j]].astype(f32)
        root, shift = unpack(total)
        turned = (root + shift).astype(bf16)
        mean = mean_ref[t]
        hi = mean.astype(bf16).astype(f32)
        mid = (mean - hi).astype(bf16).astype(f32)
        thirds = jnp.concatenate(
            [hi, mid, mean - hi - mid, jnp.zeros((TAIL - 3, cells), f32)], axis=0
        ).astype(bf16)
        moved = lax.dot_general(
            pert_ref[t], turned, (((1,), (1,)), ((), ())), preferred_element_type=f32
        )
        mean = lax.dot_general(
            thirds, ones, (((0,), (0,)), ((), ())), preferred_element_type=f32
        )
        o_ref[t] = (mean + moved).astype(bf16)


def column_of(rows):
    size = lax.axis_size("lon")
    up = [(i, (i + 2) % size) for i in range(size)]
    down = [(i, (i - 2) % size) for i in range(size)]
    cut = rows.shape[0] // 2

    def send(x, pairs):
        return lax.ppermute(x, "lon", pairs)

    def swap(x):
        return lax.ppermute(x, "lon", [(i, i ^ 1) for i in range(size)])

    below = send(rows, up)
    above = send(rows, down)
    far_a = send(below[:cut], up)
    far_b = send(above[cut:], down)
    near = [rows, below, above]
    far = [far_a, far_b]
    return near + [swap(x) for x in near] + far + [swap(x) for x in far]


def place_of(apart, other):
    near = jnp.where(apart == 0, 0, jnp.where(apart == 1, 2, 1)) + 3 * other
    return jnp.where(apart == 2, 6 + other, near)


def turn(stage, k, chips):
    pairs = []
    for lon in range(2 * chips):
        for x in range(SIDE):
            for y in range(SIDE):
                if (lon + stage) % 2 == 0:
                    to = x * SIDE + (y + k) % SIDE
                else:
                    to = (x + k) % SIDE * SIDE + y
                start = lon * SIDE * SIDE
                pairs.append((start + x * SIDE + y, start + to))
    return pairs


def local(
    obs_rows,
    innovations,
    obs_home,
    obs_lists,
    loc_weights,
    state_mean,
    state_perturb,
    interp_ids,
    interp_wts,
):
    lon_count = lax.axis_size("lon")
    lat_count = lax.axis_size("lat")
    lon = lax.axis_index("lon")
    lat = lax.axis_index("lat")
    held, obs_count, members = obs_rows.shape
    half = members // 2
    point_rows, point_cols, list_len = obs_lists.shape
    points = point_rows * point_cols
    ranks = 2 * lon_count
    column_blocks = lon_count * held

    pieces = column_of(obs_rows)
    project = jnp.einsum("lok,lo->lk", obs_rows, innovations, preferred_element_type=f32)
    column_proj = lax.all_to_all(
        jnp.broadcast_to(project, (lon_count, held, members)), "lon", 0, 0, tiled=True
    ).reshape(column_blocks, members)

    ids = obs_lists.reshape(points, list_len)
    live = ids >= 0
    home = jnp.take(obs_home, jnp.maximum(ids, 0))
    column = jnp.where(live, home // held % lat_count, lat_count)
    slot = home // (held * lat_count) * held + home % held
    mask = column[None] == jnp.arange(lat_count, dtype=jnp.int32)[:, None, None]
    rank = jnp.cumsum(mask.astype(jnp.int32), axis=2) - 1
    chosen = mask[..., None] & (rank[..., None] == jnp.arange(ranks, dtype=jnp.int32))
    slots_f = jnp.sum(jnp.where(chosen, slot.astype(f32)[None, :, :, None], 0.0), axis=2)
    wts_f = jnp.sum(
        jnp.where(chosen, loc_weights.reshape(1, points, list_len, 1), 0.0), axis=2
    )
    counts = jnp.sum(mask.astype(f32), axis=2)
    asked = jnp.concatenate(
        [
            slots_f.reshape(lat_count, points * ranks),
            counts,
            wts_f.reshape(lat_count, points * ranks),
        ],
        axis=1,
    )
    asked = lax.all_to_all(asked, "lat", 0, 0, tiled=True)
    cut = points * ranks + points
    wts = asked[:, cut:]
    named = asked[:, : points * ranks].astype(jnp.int32)
    from_lon = named // held
    apart = (from_lon // 2 - lon // 2) % (lon_count // 2)
    other = (from_lon + lon) % 2
    slots = jnp.concatenate(
        [
            place_of(apart, other) * held + named % held,
            asked[:, points * ranks : cut].astype(jnp.int32),
        ],
        axis=1,
    )

    spread = jnp.sum(
        jnp.where(
            named.reshape(lat_count * points, ranks, 1)
            == jnp.arange(column_blocks, dtype=jnp.int32),
            wts.reshape(lat_count * points, ranks, 1),
            0.0,
        ),
        axis=1,
    )
    drive = jnp.dot(spread, column_proj, precision=highest)
    drive_hi = drive.astype(bf16).astype(f32)
    drive_rows = jnp.concatenate(
        [v.reshape(lat_count, points, 2, half) for v in (drive_hi, drive - drive_hi)], axis=2
    )

    smem = pl.BlockSpec(memory_space=pltpu.SMEM)
    vmem = pl.BlockSpec(memory_space=pltpu.VMEM)
    rows = members + TAIL
    x, y = lat // SIDE, lat % SIDE
    others = jnp.arange(SIDE, dtype=jnp.int32)
    y_first = lon % 2 == 0

    def gram(k):
        order = jnp.where(
            y_first,
            (x + others) % SIDE * SIDE + (y + k) % SIDE,
            (x + k) % SIDE * SIDE + (y + others) % SIDE,
        )
        return pl.pallas_call(
            functools.partial(gram_kernel, points, ranks),
            grid=(SIDE,),
            out_shape=jax.ShapeDtypeStruct((SIDE, points, rows, half), bf16),
            in_specs=[smem, smem, smem, vmem]
            + [pl.BlockSpec(memory_space=pl.ANY)] * len(pieces),
            out_specs=pl.BlockSpec((1, points, rows, half), lambda i: (i, 0, 0, 0)),
            scratch_shapes=[
                pltpu.VMEM((points, members, members), f32),
                pltpu.VMEM((column_blocks, obs_count, members), bf16),
                pltpu.SemaphoreType.DMA((len(pieces),)),
            ],
            compiler_params=pltpu.CompilerParams(vmem_limit_bytes=2 * GRANT),
            cost_estimate=pl.CostEstimate(
                flops=2 * 16 * 512 * 256 * 256, bytes_accessed=10 << 20, transcendentals=0
            ),
            name="gram",
        )(order, slots, wts, drive_rows, *pieces)

    chips = lon_count // 2
    axes = ("lon", "lat")
    got = {}
    for k in (3, 1, 2):
        got[k] = lax.ppermute(gram(k), axes, turn(0, k, chips))
    got[0] = gram(0)

    def total(k):
        sums = got[0][k].astype(f32)
        for part in (2, 1, 3):
            sums = sums + got[part][k].astype(f32)
        return sums

    own = total(0)
    seconds = [
        lax.ppermute(total(k).astype(bf16), axes, turn(1, k, chips)) for k in (2, 1, 3)
    ]

    col = jax.ShapeDtypeStruct((point_rows, rows, half), bf16)
    whole = pl.BlockSpec((points, rows, half), lambda i: (0, 0, 0))
    col_a, col_b = pl.pallas_call(
        root_kernel,
        grid=(1,),
        out_shape=(col, col),
        in_specs=[whole] * (1 + len(seconds)),
        out_specs=(pl.BlockSpec((point_rows, rows, half), lambda i: (0, 0, 0)),) * 2,
        compiler_params=pltpu.CompilerParams(vmem_limit_bytes=2 * GRANT),
        cost_estimate=pl.CostEstimate(
            flops=4 * 12 * 2 * 256**3, bytes_accessed=2 << 20, transcendentals=0
        ),
        name="root",
    )(own, *seconds)

    right = lax.ppermute(col_a, "lat", [(i + 1, i) for i in range(lat_count - 1)])
    left = lax.ppermute(col_b, "lat", [(i, i + 1) for i in range(lat_count - 1)])
    cols = [left, col_a, col_b, right]
    top = jnp.stack([c[0] for c in cols])
    bottom = jnp.stack([c[1] for c in cols])
    inside = lax.ppermute(
        jnp.where(y_first, bottom, top), "lon", [(i, i ^ 1) for i in range(lon_count)]
    )
    outside = lax.ppermute(
        jnp.where(y_first, top, bottom),
        "lon",
        [(i, (i ^ 1) + (2 if i % 2 else -2)) for i in range(1, lon_count - 1)],
    )
    held_w = jnp.concatenate([top, bottom, inside, outside], axis=0)

    grid_cols = point_cols * lat_count
    tile_rows, tile_cols, cells = state_mean.shape
    tiles = tile_rows * tile_cols
    target_ids = interp_ids.reshape(tiles, 4)
    local_row = target_ids // grid_cols - lon * point_rows
    local_col = target_ids % grid_cols - lat * point_cols + 1
    block = jnp.where(
        local_row < 0,
        jnp.where(y_first, 3, 2),
        jnp.where(local_row >= point_rows, jnp.where(y_first, 2, 3), local_row),
    )
    places = block * 4 + local_col
    per = 4
    result = pl.pallas_call(
        state_kernel,
        grid=(tiles // per,),
        out_shape=jax.ShapeDtypeStruct((tiles, cells, members), bf16),
        in_specs=[
            smem,
            smem,
            pl.BlockSpec((per, 1, cells), lambda i: (i, 0, 0)),
            pl.BlockSpec((per, cells, members), lambda i: (i, 0, 0)),
            vmem,
        ],
        out_specs=pl.BlockSpec((per, cells, members), lambda i: (i, 0, 0)),
        compiler_params=pltpu.CompilerParams(vmem_limit_bytes=GRANT),
        cost_estimate=pl.CostEstimate(
            flops=2 * 16 * 512 * 256 * 256, bytes_accessed=11 << 20, transcendentals=0
        ),
        name="state",
    )(
        places,
        interp_wts.reshape(tiles, 4),
        state_mean.reshape(tiles, 1, cells),
        state_perturb.reshape(tiles, cells, members),
        held_w,
    )
    return result.reshape(tile_rows, tile_cols, cells, members)


def solution(mesh):
    return jax.shard_map(
        local,
        mesh=mesh,
        in_specs=(
            P(("lon", "lat"), None, None),
            P(("lon", "lat"), None),
            P(),
            P("lon", "lat", None),
            P("lon", "lat", None),
            P("lon", "lat", None),
            P("lon", "lat", None, None),
            P("lon", "lat", None),
            P("lon", "lat", None),
        ),
        out_specs=P("lon", "lat", None, None),
        check_vma=False,
    )
```

```python
import functools

import jax
import jax.numpy as jnp
from jax import lax
from jax.experimental import pallas as pl
from jax.experimental.pallas import tpu as pltpu
from jax.sharding import PartitionSpec as P

ITERS = 5
FAST = 4
TAIL = 16
SIDE = 4
GRANT = 8 << 20
bf16 = jnp.bfloat16
f32 = jnp.float32
highest = lax.Precision.HIGHEST


def product(a, b):
    rest = jnp.dot(a[1].astype(bf16), b[1].astype(bf16), preferred_element_type=f32)
    return a[0] * b[0], a[0] * b[1] + b[0] * a[1] + rest


def step_factor(a):
    return 1.5 - 0.5 * a[0], -0.5 * a[1]


def row_times(vector, a):
    hi = vector.astype(bf16).astype(f32)
    rows = jnp.concatenate([hi, vector - hi, jnp.zeros((14, vector.shape[1]), f32)], axis=0)
    got = jnp.dot(rows.astype(bf16), a[1].astype(bf16), preferred_element_type=f32)
    return a[0] * vector + jnp.sum(got[:2], axis=0, keepdims=True)


def places_of(half):
    row = lax.broadcasted_iota(jnp.int32, (half, half), 0)
    col = lax.broadcasted_iota(jnp.int32, (half, half), 1)
    return row, col


def pack(matrix, vector_rows):
    half = matrix.shape[0] // 2
    row, col = places_of(half)
    lower_right = matrix[half:, half:]
    both = jnp.where(row >= col, matrix[:half, :half], lower_right)
    diagonal = jnp.sum(jnp.where(row == col, lower_right, 0.0), axis=0, keepdims=True)
    hi = diagonal.astype(bf16).astype(f32)
    tail = jnp.concatenate(
        [hi, diagonal - hi, vector_rows, jnp.zeros((TAIL - 6, half), f32)], axis=0
    )
    return matrix[half:, :half].astype(bf16), both.astype(bf16), tail.astype(bf16)


def unpack(total):
    half = total.shape[1]
    members = 2 * half
    row, col = places_of(half)
    corner = total[:half]
    both = total[half:members]
    turned = both.T
    diagonal = total[members : members + 1] + total[members + 1 : members + 2]
    upper_left = jnp.where(row >= col, both, turned)
    lower_right = jnp.where(
        row == col, jnp.broadcast_to(diagonal, (half, half)), jnp.where(row < col, both, turned)
    )
    matrix = jnp.concatenate(
        [
            jnp.concatenate([upper_left, corner.T], axis=1),
            jnp.concatenate([corner, lower_right], axis=1),
        ],
        axis=0,
    )
    vector = jnp.concatenate(
        [
            total[members + 2 + h : members + 3 + h] + total[members + 4 + h : members + 5 + h]
            for h in range(2)
        ],
        axis=1,
    )
    return matrix, vector


def vector_rows(vector, half):
    hi = vector.astype(bf16).astype(f32)
    lo = vector - hi
    return jnp.concatenate([hi[:, :half], hi[:, half:], lo[:, :half], lo[:, half:]], axis=0)


def join_kernel(start, *refs):
    pieces, (y_ref, sem) = refs[:-2], refs[-2:]
    copies = []
    at = start
    for i, piece in enumerate(pieces):
        copies.append(
            pltpu.make_async_copy(piece, y_ref.at[pl.ds(at, piece.shape[0])], sem.at[i])
        )
        copies[-1].start()
        at += piece.shape[0]
    for copy in copies:
        copy.wait()


def gram_kernel(points, ranks, order, slots, wts, drive_ref, y_ref, o_ref, acc_ref):
    dest = order[pl.program_id(0)]
    half = y_ref.shape[2] // 2
    most = jnp.int32(0)
    for p in range(points):
        at = p * ranks
        ys = [y_ref[slots[dest, at + k]] for k in range(FAST)]
        yw = [(ys[k].astype(f32) * wts[dest, at + k]).astype(bf16) for k in range(FAST)]
        acc_ref[p] = lax.dot_general(
            jnp.concatenate(yw, axis=0),
            jnp.concatenate(ys, axis=0),
            (((0,), (0,)), ((), ())),
            preferred_element_type=f32,
        )
        most = jnp.maximum(most, slots[dest, points * ranks + p])

    @pl.when(most > FAST)
    def _():
        for p in range(points):
            at = p * ranks

            @pl.loop(FAST, jnp.maximum(slots[dest, points * ranks + p], FAST))
            def _(k):
                y = y_ref[slots[dest, at + k]]
                w = (y.astype(f32) * wts[dest, at + k]).astype(bf16)
                acc_ref[p] += lax.dot_general(
                    w, y, (((0,), (0,)), ((), ())), preferred_element_type=f32
                )

    for p in range(points):
        corner, both, tail = pack(acc_ref[p], drive_ref[dest, p])
        o_ref[0, p, :half] = corner
        o_ref[0, p, half : 2 * half] = both
        o_ref[0, p, 2 * half :] = tail


def root_kernel(odd, *refs):
    parts, outs = refs[:-2], refs[-2:]
    points, rows, half = parts[0].shape
    members = 2 * half
    here = range(points)
    eye = (
        lax.broadcasted_iota(jnp.int32, (members, members), 0)
        == lax.broadcasted_iota(jnp.int32, (members, members), 1)
    ).astype(f32)
    scale = 1.0 / (members - 1)
    drives, bounds, uppers, lowers = [], [], [], []
    for p in here:
        total = parts[0][p].astype(f32)
        for part in parts[1:]:
            total = total + part[p].astype(f32)
        cov, drive = unpack(total)
        drives.append(drive * scale)
        system = eye + cov * scale
        bound = jnp.max(
            jnp.sum(jnp.abs(system), axis=0, keepdims=True), axis=1, keepdims=True
        )
        trace = jnp.sum(
            jnp.sum(system * eye, axis=0, keepdims=True), axis=1, keepdims=True
        )
        level = trace * (1.0 / members)
        inverse = 1.0 / bound
        bounds.append(bound)
        uppers.append((level * inverse, (system - level * eye) * inverse))
    lowers = [step_factor(uppers[p]) for p in here]
    uppers = [product(uppers[p], lowers[p]) for p in here]
    for sweep in range(1, ITERS):
        factors = [step_factor(product(lowers[p], uppers[p])) for p in here]
        if sweep < ITERS - 1:
            uppers = [product(uppers[p], factors[p]) for p in here]
        lowers = [product(factors[p], lowers[p]) for p in here]
    for p in here:
        norm = lax.rsqrt(bounds[p])
        root = (lowers[p][0] * norm, lowers[p][1] * norm)
        shift = row_times(row_times(drives[p], root), root)
        corner, both, tail = pack(root[1] + root[0] * eye, vector_rows(shift, half))
        row = p // 2
        for flip in range(2):

            @pl.when(odd[0] == flip)
            def _(o_ref=outs[(p + 1 + flip) % 2], row=row, corner=corner, both=both, tail=tail):
                o_ref[row, :half] = corner
                o_ref[row, half:members] = both
                o_ref[row, members:] = tail


def state_kernel(places, mixing, mean_ref, pert_ref, w_ref, o_ref):
    step = pl.program_id(0)
    count, cells, members = o_ref.shape
    ones = jnp.ones((TAIL, members), bf16)
    for t in range(count):
        tile = step * count + t
        total = mixing[tile, 0] * w_ref[places[tile, 0]].astype(f32)
        for j in range(1, 4):
            total = total + mixing[tile, j] * w_ref[places[tile, j]].astype(f32)
        root, shift = unpack(total)
        turned = (root + shift).astype(bf16)
        mean = mean_ref[t]
        hi = mean.astype(bf16).astype(f32)
        mid = (mean - hi).astype(bf16).astype(f32)
        thirds = jnp.concatenate(
            [hi, mid, mean - hi - mid, jnp.zeros((TAIL - 3, cells), f32)], axis=0
        ).astype(bf16)
        moved = lax.dot_general(
            pert_ref[t], turned, (((1,), (1,)), ((), ())), preferred_element_type=f32
        )
        mean = lax.dot_general(
            thirds, ones, (((0,), (0,)), ((), ())), preferred_element_type=f32
        )
        o_ref[t] = (mean + moved).astype(bf16)


def column_of(rows):
    size = lax.axis_size("lon")
    up = [(i, (i + 2) % size) for i in range(size)]
    down = [(i, (i - 2) % size) for i in range(size)]
    cut = rows.shape[0] // 2

    def send(x, pairs):
        return lax.ppermute(x, "lon", pairs)

    def swap(x):
        return lax.ppermute(x, "lon", [(i, i ^ 1) for i in range(size)])

    below = send(rows, up)
    above = send(rows, down)
    far_a = send(below[:cut], up)
    far_b = send(above[cut:], down)
    near = [rows, below, above]
    far = [far_a, far_b]
    return near + [swap(x) for x in near] + far + [swap(x) for x in far]


def place_of(apart, other):
    near = jnp.where(apart == 0, 0, jnp.where(apart == 1, 2, 1)) + 3 * other
    return jnp.where(apart == 2, 6 + other, near)


def turn(stage, k, chips):
    pairs = []
    for lon in range(2 * chips):
        for x in range(SIDE):
            for y in range(SIDE):
                if (lon + stage) % 2 == 0:
                    to = x * SIDE + (y + k) % SIDE
                else:
                    to = (x + k) % SIDE * SIDE + y
                start = lon * SIDE * SIDE
                pairs.append((start + x * SIDE + y, start + to))
    return pairs


def local(
    obs_rows,
    innovations,
    obs_home,
    obs_lists,
    loc_weights,
    state_mean,
    state_perturb,
    interp_ids,
    interp_wts,
):
    lon_count = lax.axis_size("lon")
    lat_count = lax.axis_size("lat")
    lon = lax.axis_index("lon")
    lat = lax.axis_index("lat")
    held, obs_count, members = obs_rows.shape
    half = members // 2
    point_rows, point_cols, list_len = obs_lists.shape
    points = point_rows * point_cols
    ranks = 2 * lon_count
    column_blocks = lon_count * held

    pieces = column_of(obs_rows)
    project = jnp.einsum("lok,lo->lk", obs_rows, innovations, preferred_element_type=f32)
    column_proj = lax.all_to_all(
        jnp.broadcast_to(project, (lon_count, held, members)), "lon", 0, 0, tiled=True
    ).reshape(column_blocks, members)

    ids = obs_lists.reshape(points, list_len)
    live = ids >= 0
    home = jnp.take(obs_home, jnp.maximum(ids, 0))
    column = jnp.where(live, home // held % lat_count, lat_count)
    slot = home // (held * lat_count) * held + home % held
    mask = column[None] == jnp.arange(lat_count, dtype=jnp.int32)[:, None, None]
    rank = jnp.cumsum(mask.astype(jnp.int32), axis=2) - 1
    chosen = mask[..., None] & (rank[..., None] == jnp.arange(ranks, dtype=jnp.int32))
    slots_f = jnp.sum(jnp.where(chosen, slot.astype(f32)[None, :, :, None], 0.0), axis=2)
    wts_f = jnp.sum(
        jnp.where(chosen, loc_weights.reshape(1, points, list_len, 1), 0.0), axis=2
    )
    counts = jnp.sum(mask.astype(f32), axis=2)
    asked = jnp.concatenate(
        [
            slots_f.reshape(lat_count, points * ranks),
            counts,
            wts_f.reshape(lat_count, points * ranks),
        ],
        axis=1,
    )
    asked = lax.all_to_all(asked, "lat", 0, 0, tiled=True)
    cut = points * ranks + points
    wts = asked[:, cut:]
    named = asked[:, : points * ranks].astype(jnp.int32)
    from_lon = named // held
    apart = (from_lon // 2 - lon // 2) % (lon_count // 2)
    other = (from_lon + lon) % 2
    slots = jnp.concatenate(
        [
            place_of(apart, other) * held + named % held,
            asked[:, points * ranks : cut].astype(jnp.int32),
        ],
        axis=1,
    )

    spread = jnp.sum(
        jnp.where(
            named.reshape(lat_count * points, ranks, 1)
            == jnp.arange(column_blocks, dtype=jnp.int32),
            wts.reshape(lat_count * points, ranks, 1),
            0.0,
        ),
        axis=1,
    )
    drive = jnp.dot(spread, column_proj, precision=highest)
    drive_hi = drive.astype(bf16).astype(f32)
    drive_rows = jnp.concatenate(
        [v.reshape(lat_count, points, 2, half) for v in (drive_hi, drive - drive_hi)], axis=2
    )

    smem = pl.BlockSpec(memory_space=pltpu.SMEM)
    vmem = pl.BlockSpec(memory_space=pltpu.VMEM)
    rows = members + TAIL
    x, y = lat // SIDE, lat % SIDE
    others = jnp.arange(SIDE, dtype=jnp.int32)
    y_first = lon % 2 == 0

    def gram(k):
        order = jnp.where(
            y_first,
            (x + others) % SIDE * SIDE + (y + k) % SIDE,
            (x + k) % SIDE * SIDE + (y + others) % SIDE,
        )
        return pl.pallas_call(
            functools.partial(gram_kernel, points, ranks),
            grid=(SIDE,),
            out_shape=jax.ShapeDtypeStruct((SIDE, points, rows, half), bf16),
            in_specs=[smem, smem, smem, vmem, vmem],
            out_specs=pl.BlockSpec((1, points, rows, half), lambda i: (i, 0, 0, 0)),
            scratch_shapes=[
                pltpu.VMEM((points, members, members), f32),
            ],
            compiler_params=pltpu.CompilerParams(vmem_limit_bytes=GRANT),
            cost_estimate=pl.CostEstimate(
                flops=2 * 16 * 512 * 256 * 256, bytes_accessed=10 << 20, transcendentals=0
            ),
            name="gram",
        )(order, slots, wts, drive_rows, column_rows)

    chips = lon_count // 2
    column_rows = pl.pallas_call(
        functools.partial(join_kernel, 0),
        out_shape=jax.ShapeDtypeStruct((column_blocks, obs_count, members), bf16),
        in_specs=[pl.BlockSpec(memory_space=pl.ANY)] * len(pieces),
        out_specs=pl.BlockSpec(memory_space=pl.ANY),
        scratch_shapes=[pltpu.SemaphoreType.DMA((len(pieces),))],
        compiler_params=pltpu.CompilerParams(vmem_limit_bytes=1 << 20),
        name="join",
    )(*pieces)
    axes = ("lon", "lat")
    got = {}
    for k in (3, 1, 2):
        got[k] = lax.ppermute(gram(k), axes, turn(0, k, chips))
    got[0] = gram(0)

    def total(k):
        sums = got[0][k].astype(f32)
        for part in (2, 1, 3):
            sums = sums + got[part][k].astype(f32)
        return sums

    own = total(0)
    seconds = [
        lax.ppermute(total(k).astype(bf16), axes, turn(1, k, chips)) for k in (2, 1, 3)
    ]

    col = jax.ShapeDtypeStruct((point_rows, rows, half), bf16)
    whole = pl.BlockSpec((points, rows, half), lambda i: (0, 0, 0))
    odd = lat % 2 == 1
    near_col, other_col = pl.pallas_call(
        root_kernel,
        grid=(1,),
        out_shape=(col, col),
        in_specs=[smem] + [whole] * (1 + len(seconds)),
        out_specs=(pl.BlockSpec((point_rows, rows, half), lambda i: (0, 0, 0)),) * 2,
        compiler_params=pltpu.CompilerParams(vmem_limit_bytes=16 << 20),
        cost_estimate=pl.CostEstimate(
            flops=4 * 12 * 2 * 256**3, bytes_accessed=2 << 20, transcendentals=0
        ),
        name="root",
    )((lat % 2).astype(jnp.int32).reshape(1), own, *seconds)

    near_got = lax.ppermute(near_col, "lat", [(i, i ^ 1) for i in range(lat_count)])
    other_got = lax.ppermute(
        other_col, "lat", [(i, (i - 1 ^ 1) + 1) for i in range(1, lat_count - 1)]
    )
    cols = [other_got, other_col, near_col, near_got]
    top = jnp.stack([c[0] for c in cols])
    bottom = jnp.stack([c[1] for c in cols])
    inside = lax.ppermute(
        jnp.where(y_first, bottom, top), "lon", [(i, i ^ 1) for i in range(lon_count)]
    )
    outside = lax.ppermute(
        jnp.where(y_first, top, bottom),
        "lon",
        [(i, (i ^ 1) + (2 if i % 2 else -2)) for i in range(1, lon_count - 1)],
    )
    held_w = jnp.concatenate([top, bottom, inside, outside], axis=0)

    grid_cols = point_cols * lat_count
    tile_rows, tile_cols, cells = state_mean.shape
    tiles = tile_rows * tile_cols
    target_ids = interp_ids.reshape(tiles, 4)
    local_row = target_ids // grid_cols - lon * point_rows
    local_col = target_ids % grid_cols - lat * point_cols + 1
    block = jnp.where(
        local_row < 0,
        jnp.where(y_first, 3, 2),
        jnp.where(local_row >= point_rows, jnp.where(y_first, 2, 3), local_row),
    )
    places = block * 4 + jnp.where(odd, 3 - local_col, local_col)
    per = 4
    result = pl.pallas_call(
        state_kernel,
        grid=(tiles // per,),
        out_shape=jax.ShapeDtypeStruct((tiles, cells, members), bf16),
        in_specs=[
            smem,
            smem,
            pl.BlockSpec((per, 1, cells), lambda i: (i, 0, 0)),
            pl.BlockSpec((per, cells, members), lambda i: (i, 0, 0)),
            vmem,
        ],
        out_specs=pl.BlockSpec((per, cells, members), lambda i: (i, 0, 0)),
        compiler_params=pltpu.CompilerParams(vmem_limit_bytes=12 << 20),
        cost_estimate=pl.CostEstimate(
            flops=2 * 16 * 512 * 256 * 256, bytes_accessed=11 << 20, transcendentals=0
        ),
        name="state",
    )(
        places,
        interp_wts.reshape(tiles, 4),
        state_mean.reshape(tiles, 1, cells),
        state_perturb.reshape(tiles, cells, members),
        held_w,
    )
    return result.reshape(tile_rows, tile_cols, cells, members)


def solution(mesh):
    return jax.shard_map(
        local,
        mesh=mesh,
        in_specs=(
            P(("lon", "lat"), None, None),
            P(("lon", "lat"), None),
            P(),
            P("lon", "lat", None),
            P("lon", "lat", None),
            P("lon", "lat", None),
            P("lon", "lat", None, None),
            P("lon", "lat", None),
            P("lon", "lat", None),
        ),
        out_specs=P("lon", "lat", None, None),
        check_vma=False,
    )
```

```python
import functools

import jax
import jax.numpy as jnp
from jax import lax
from jax.experimental import pallas as pl
from jax.experimental.pallas import tpu as pltpu
from jax.sharding import PartitionSpec as P

ITERS = 5
FAST = 4
TAIL = 16
SIDE = 4
GRANT = 8 << 20
bf16 = jnp.bfloat16
f32 = jnp.float32
highest = lax.Precision.HIGHEST


def product(a, b):
    rest = jnp.dot(a[1].astype(bf16), b[1].astype(bf16), preferred_element_type=f32)
    return a[0] * b[0], a[0] * b[1] + b[0] * a[1] + rest


def step_factor(a):
    return 1.5 - 0.5 * a[0], -0.5 * a[1]


def row_times(vector, a):
    hi = vector.astype(bf16).astype(f32)
    rows = jnp.concatenate([hi, vector - hi, jnp.zeros((14, vector.shape[1]), f32)], axis=0)
    got = jnp.dot(rows.astype(bf16), a[1].astype(bf16), preferred_element_type=f32)
    return a[0] * vector + jnp.sum(got[:2], axis=0, keepdims=True)


def places_of(half):
    row = lax.broadcasted_iota(jnp.int32, (half, half), 0)
    col = lax.broadcasted_iota(jnp.int32, (half, half), 1)
    return row, col


def pack(matrix, vector_rows):
    half = matrix.shape[0] // 2
    row, col = places_of(half)
    lower_right = matrix[half:, half:]
    both = jnp.where(row >= col, matrix[:half, :half], lower_right)
    diagonal = jnp.sum(jnp.where(row == col, lower_right, 0.0), axis=0, keepdims=True)
    hi = diagonal.astype(bf16).astype(f32)
    tail = jnp.concatenate(
        [hi, diagonal - hi, vector_rows, jnp.zeros((TAIL - 6, half), f32)], axis=0
    )
    return matrix[half:, :half], both, tail


def unpack(total):
    half = total.shape[1]
    members = 2 * half
    row, col = places_of(half)
    corner = total[:half]
    both = total[half:members]
    turned = both.T
    diagonal = total[members : members + 1] + total[members + 1 : members + 2]
    upper_left = jnp.where(row >= col, both, turned)
    lower_right = jnp.where(
        row == col, jnp.broadcast_to(diagonal, (half, half)), jnp.where(row < col, both, turned)
    )
    matrix = jnp.concatenate(
        [
            jnp.concatenate([upper_left, corner.T], axis=1),
            jnp.concatenate([corner, lower_right], axis=1),
        ],
        axis=0,
    )
    vector = jnp.concatenate(
        [
            total[members + 2 + h : members + 3 + h] + total[members + 4 + h : members + 5 + h]
            for h in range(2)
        ],
        axis=1,
    )
    return matrix, vector


def vector_rows(vector, half):
    hi = vector.astype(bf16).astype(f32)
    lo = vector - hi
    return jnp.concatenate([hi[:, :half], hi[:, half:], lo[:, :half], lo[:, half:]], axis=0)


def join_kernel(start, *refs):
    pieces, (y_ref, sem) = refs[:-2], refs[-2:]
    copies = []
    at = start
    for i, piece in enumerate(pieces):
        copies.append(
            pltpu.make_async_copy(piece, y_ref.at[pl.ds(at, piece.shape[0])], sem.at[i])
        )
        copies[-1].start()
        at += piece.shape[0]
    for copy in copies:
        copy.wait()


def gram_kernel(points, ranks, order, slots, wts, drive_ref, y_ref, *refs):
    added, (o_ref, acc_ref) = refs[:-2], refs[-2:]
    dest = order[pl.program_id(0)]
    half = y_ref.shape[2] // 2
    most = jnp.int32(0)
    for p in range(points):
        at = p * ranks
        ys = [y_ref[slots[dest, at + k]] for k in range(FAST)]
        yw = [(ys[k].astype(f32) * wts[dest, at + k]).astype(bf16) for k in range(FAST)]
        acc_ref[p] = lax.dot_general(
            jnp.concatenate(yw, axis=0),
            jnp.concatenate(ys, axis=0),
            (((0,), (0,)), ((), ())),
            preferred_element_type=f32,
        )
        most = jnp.maximum(most, slots[dest, points * ranks + p])

    @pl.when(most > FAST)
    def _():
        for p in range(points):
            at = p * ranks

            @pl.loop(FAST, jnp.maximum(slots[dest, points * ranks + p], FAST))
            def _(k):
                y = y_ref[slots[dest, at + k]]
                w = (y.astype(f32) * wts[dest, at + k]).astype(bf16)
                acc_ref[p] += lax.dot_general(
                    w, y, (((0,), (0,)), ((), ())), preferred_element_type=f32
                )

    for p in range(points):
        packed = pack(acc_ref[p], drive_ref[dest, p])
        for i, part in enumerate(packed):
            at = pl.ds(i * half, part.shape[0])
            for ref in added:
                part = part + ref[0, p, at].astype(f32)
            o_ref[0, p, at] = part.astype(bf16)


def root_kernel(odd, *refs):
    parts, outs = refs[:-2], refs[-2:]
    points, rows, half = parts[0].shape
    members = 2 * half
    here = range(points)
    eye = (
        lax.broadcasted_iota(jnp.int32, (members, members), 0)
        == lax.broadcasted_iota(jnp.int32, (members, members), 1)
    ).astype(f32)
    scale = 1.0 / (members - 1)
    drives, bounds, uppers, lowers = [], [], [], []
    for p in here:
        total = parts[0][p].astype(f32)
        for part in parts[1:]:
            total = total + part[p].astype(f32)
        cov, drive = unpack(total)
        drives.append(drive * scale)
        system = eye + cov * scale
        bound = jnp.max(
            jnp.sum(jnp.abs(system), axis=0, keepdims=True), axis=1, keepdims=True
        )
        trace = jnp.sum(
            jnp.sum(system * eye, axis=0, keepdims=True), axis=1, keepdims=True
        )
        level = trace * (1.0 / members)
        inverse = 1.0 / bound
        bounds.append(bound)
        uppers.append((level * inverse, (system - level * eye) * inverse))
    lowers = [step_factor(uppers[p]) for p in here]
    uppers = [product(uppers[p], lowers[p]) for p in here]
    for sweep in range(1, ITERS):
        factors = [step_factor(product(lowers[p], uppers[p])) for p in here]
        if sweep < ITERS - 1:
            uppers = [product(uppers[p], factors[p]) for p in here]
        lowers = [product(factors[p], lowers[p]) for p in here]
    for p in here:
        norm = lax.rsqrt(bounds[p])
        root = (lowers[p][0] * norm, lowers[p][1] * norm)
        shift = row_times(row_times(drives[p], root), root)
        corner, both, tail = (
            v.astype(bf16) for v in pack(root[1] + root[0] * eye, vector_rows(shift, half))
        )
        row = p // 2
        for flip in range(2):

            @pl.when(odd[0] == flip)
            def _(o_ref=outs[(p + 1 + flip) % 2], row=row, corner=corner, both=both, tail=tail):
                o_ref[row, :half] = corner
                o_ref[row, half:members] = both
                o_ref[row, members:] = tail


def state_kernel(places, mixing, mean_ref, pert_ref, w_ref, o_ref):
    step = pl.program_id(0)
    count, cells, members = o_ref.shape
    ones = jnp.ones((TAIL, members), bf16)
    for t in range(count):
        tile = step * count + t
        total = mixing[tile, 0] * w_ref[places[tile, 0]].astype(f32)
        for j in range(1, 4):
            total = total + mixing[tile, j] * w_ref[places[tile, j]].astype(f32)
        root, shift = unpack(total)
        turned = (root + shift).astype(bf16)
        mean = mean_ref[t]
        hi = mean.astype(bf16).astype(f32)
        mid = (mean - hi).astype(bf16).astype(f32)
        thirds = jnp.concatenate(
            [hi, mid, mean - hi - mid, jnp.zeros((TAIL - 3, cells), f32)], axis=0
        ).astype(bf16)
        moved = lax.dot_general(
            pert_ref[t], turned, (((1,), (1,)), ((), ())), preferred_element_type=f32
        )
        mean = lax.dot_general(
            thirds, ones, (((0,), (0,)), ((), ())), preferred_element_type=f32
        )
        o_ref[t] = (mean + moved).astype(bf16)


def column_of(rows):
    size = lax.axis_size("lon")
    up = [(i, (i + 2) % size) for i in range(size)]
    down = [(i, (i - 2) % size) for i in range(size)]
    cut = rows.shape[0] // 2

    def send(x, pairs):
        return lax.ppermute(x, "lon", pairs)

    def swap(x):
        return lax.ppermute(x, "lon", [(i, i ^ 1) for i in range(size)])

    below = send(rows, up)
    above = send(rows, down)
    far_a = send(below[:cut], up)
    far_b = send(above[cut:], down)
    near = [rows, below, above]
    far = [far_a, far_b]
    return near + [swap(x) for x in near] + far + [swap(x) for x in far]


def place_of(apart, other):
    near = jnp.where(apart == 0, 0, jnp.where(apart == 1, 2, 1)) + 3 * other
    return jnp.where(apart == 2, 6 + other, near)


def turn(stage, k, chips):
    pairs = []
    for lon in range(2 * chips):
        for x in range(SIDE):
            for y in range(SIDE):
                if (lon + stage) % 2 == 0:
                    to = x * SIDE + (y + k) % SIDE
                else:
                    to = (x + k) % SIDE * SIDE + y
                start = lon * SIDE * SIDE
                pairs.append((start + x * SIDE + y, start + to))
    return pairs


def local(
    obs_rows,
    innovations,
    obs_home,
    obs_lists,
    loc_weights,
    state_mean,
    state_perturb,
    interp_ids,
    interp_wts,
):
    lon_count = lax.axis_size("lon")
    lat_count = lax.axis_size("lat")
    lon = lax.axis_index("lon")
    lat = lax.axis_index("lat")
    held, obs_count, members = obs_rows.shape
    half = members // 2
    point_rows, point_cols, list_len = obs_lists.shape
    points = point_rows * point_cols
    ranks = 2 * lon_count
    column_blocks = lon_count * held

    pieces = column_of(obs_rows)
    innovations, _, _ = lax.optimization_barrier((innovations, pieces[1], pieces[2]))
    project = jnp.einsum("lok,lo->lk", obs_rows, innovations, preferred_element_type=f32)
    column_proj = lax.all_to_all(
        jnp.broadcast_to(project, (lon_count, held, members)), "lon", 0, 0, tiled=True
    ).reshape(column_blocks, members)

    ids = obs_lists.reshape(points, list_len)
    live = ids >= 0
    home = jnp.take(obs_home, jnp.maximum(ids, 0))
    column = jnp.where(live, home // held % lat_count, lat_count)
    slot = home // (held * lat_count) * held + home % held
    mask = column[None] == jnp.arange(lat_count, dtype=jnp.int32)[:, None, None]
    rank = jnp.cumsum(mask.astype(jnp.int32), axis=2) - 1
    chosen = mask[..., None] & (rank[..., None] == jnp.arange(ranks, dtype=jnp.int32))
    slots_f = jnp.sum(jnp.where(chosen, slot.astype(f32)[None, :, :, None], 0.0), axis=2)
    wts_f = jnp.sum(
        jnp.where(chosen, loc_weights.reshape(1, points, list_len, 1), 0.0), axis=2
    )
    counts = jnp.sum(mask.astype(f32), axis=2)
    asked = jnp.concatenate(
        [
            slots_f.reshape(lat_count, points * ranks),
            counts,
            wts_f.reshape(lat_count, points * ranks),
        ],
        axis=1,
    )
    asked = lax.all_to_all(asked, "lat", 0, 0, tiled=True)
    cut = points * ranks + points
    wts = asked[:, cut:]
    named = asked[:, : points * ranks].astype(jnp.int32)
    from_lon = named // held
    apart = (from_lon // 2 - lon // 2) % (lon_count // 2)
    other = (from_lon + lon) % 2
    slots = jnp.concatenate(
        [
            place_of(apart, other) * held + named % held,
            asked[:, points * ranks : cut].astype(jnp.int32),
        ],
        axis=1,
    )

    spread = jnp.sum(
        jnp.where(
            named.reshape(lat_count * points, ranks, 1)
            == jnp.arange(column_blocks, dtype=jnp.int32),
            wts.reshape(lat_count * points, ranks, 1),
            0.0,
        ),
        axis=1,
    )
    drive = jnp.dot(spread, column_proj, precision=highest)
    drive_hi = drive.astype(bf16).astype(f32)
    drive_rows = jnp.concatenate(
        [v.reshape(lat_count, points, 2, half) for v in (drive_hi, drive - drive_hi)], axis=2
    )

    smem = pl.BlockSpec(memory_space=pltpu.SMEM)
    vmem = pl.BlockSpec(memory_space=pltpu.VMEM)
    rows = members + TAIL
    x, y = lat // SIDE, lat % SIDE
    y_first = lon % 2 == 0

    def gram(k, ways, *added):
        others = jnp.asarray(ways, jnp.int32)
        order = jnp.where(
            y_first,
            (x + others) % SIDE * SIDE + (y + k) % SIDE,
            (x + k) % SIDE * SIDE + (y + others) % SIDE,
        )
        return pl.pallas_call(
            functools.partial(gram_kernel, points, ranks),
            grid=(len(ways),),
            out_shape=jax.ShapeDtypeStruct((len(ways), points, rows, half), bf16),
            in_specs=[smem, smem, smem, vmem, vmem]
            + [pl.BlockSpec((1, points, rows, half), lambda i: (i, 0, 0, 0))] * len(added),
            out_specs=pl.BlockSpec((1, points, rows, half), lambda i: (i, 0, 0, 0)),
            scratch_shapes=[
                pltpu.VMEM((points, members, members), f32),
            ],
            compiler_params=pltpu.CompilerParams(vmem_limit_bytes=GRANT),
            cost_estimate=pl.CostEstimate(
                flops=len(ways) * 8 * 512 * 256 * 256, bytes_accessed=len(ways) << 20, transcendentals=0
            ),
            name="gram",
        )(order, slots, wts, drive_rows, column_rows, *added)

    chips = lon_count // 2
    column_rows = pl.pallas_call(
        functools.partial(join_kernel, 0),
        out_shape=jax.ShapeDtypeStruct((column_blocks, obs_count, members), bf16),
        in_specs=[pl.BlockSpec(memory_space=pl.ANY)] * len(pieces),
        out_specs=pl.BlockSpec(memory_space=pl.ANY),
        scratch_shapes=[pltpu.SemaphoreType.DMA((len(pieces),))],
        compiler_params=pltpu.CompilerParams(vmem_limit_bytes=1 << 20),
        name="join",
    )(*pieces)
    axes = ("lon", "lat")
    def send(block, k):
        return lax.ppermute(block, axes, turn(0, k, chips))

    early, late = (0, 1), (2, 3)
    onward = send(gram(2, early), 1), send(gram(2, late), 3)
    straight = send(gram(1, late), 1), send(gram(3, early), 3)
    relayed = (
        send(gram(1, early, onward[0]), 1),
        send(gram(3, late, onward[1]), 3),
    )
    mine = gram(0, early + late)

    def total(k):
        arrived = (relayed[0], straight[1]) if k in early else (straight[0], relayed[1])
        sums = mine[k].astype(f32)
        for part in arrived:
            sums = sums + part[k % 2].astype(f32)
        return sums

    own = total(0)
    seconds = [
        lax.ppermute(total(k).astype(bf16), axes, turn(1, k, chips)) for k in (2, 1, 3)
    ]

    col = jax.ShapeDtypeStruct((point_rows, rows, half), bf16)
    whole = pl.BlockSpec((points, rows, half), lambda i: (0, 0, 0))
    odd = lat % 2 == 1
    near_col, other_col = pl.pallas_call(
        root_kernel,
        grid=(1,),
        out_shape=(col, col),
        in_specs=[smem] + [whole] * (1 + len(seconds)),
        out_specs=(pl.BlockSpec((point_rows, rows, half), lambda i: (0, 0, 0)),) * 2,
        compiler_params=pltpu.CompilerParams(vmem_limit_bytes=16 << 20),
        cost_estimate=pl.CostEstimate(
            flops=4 * 12 * 2 * 256**3, bytes_accessed=2 << 20, transcendentals=0
        ),
        name="root",
    )((lat % 2).astype(jnp.int32).reshape(1), own, *seconds)

    near_got = lax.ppermute(near_col, "lat", [(i, i ^ 1) for i in range(lat_count)])
    other_got = lax.ppermute(
        other_col, "lat", [(i, (i - 1 ^ 1) + 1) for i in range(1, lat_count - 1)]
    )
    cols = [other_got, other_col, near_col, near_got]
    top = jnp.stack([c[0] for c in cols])
    bottom = jnp.stack([c[1] for c in cols])
    inside = lax.ppermute(
        jnp.where(y_first, bottom, top), "lon", [(i, i ^ 1) for i in range(lon_count)]
    )
    outside = lax.ppermute(
        jnp.where(y_first, top, bottom),
        "lon",
        [(i, (i ^ 1) + (2 if i % 2 else -2)) for i in range(1, lon_count - 1)],
    )
    held_w = jnp.concatenate([top, bottom, inside, outside], axis=0)

    grid_cols = point_cols * lat_count
    tile_rows, tile_cols, cells = state_mean.shape
    tiles = tile_rows * tile_cols
    target_ids = interp_ids.reshape(tiles, 4)
    local_row = target_ids // grid_cols - lon * point_rows
    local_col = target_ids % grid_cols - lat * point_cols + 1
    block = jnp.where(
        local_row < 0,
        jnp.where(y_first, 3, 2),
        jnp.where(local_row >= point_rows, jnp.where(y_first, 2, 3), local_row),
    )
    places = block * 4 + jnp.where(odd, 3 - local_col, local_col)
    per = 4
    result = pl.pallas_call(
        state_kernel,
        grid=(tiles // per,),
        out_shape=jax.ShapeDtypeStruct((tiles, cells, members), bf16),
        in_specs=[
            smem,
            smem,
            pl.BlockSpec((per, 1, cells), lambda i: (i, 0, 0)),
            pl.BlockSpec((per, cells, members), lambda i: (i, 0, 0)),
            vmem,
        ],
        out_specs=pl.BlockSpec((per, cells, members), lambda i: (i, 0, 0)),
        compiler_params=pltpu.CompilerParams(vmem_limit_bytes=12 << 20),
        cost_estimate=pl.CostEstimate(
            flops=2 * 16 * 512 * 256 * 256, bytes_accessed=11 << 20, transcendentals=0
        ),
        name="state",
    )(
        places,
        interp_wts.reshape(tiles, 4),
        state_mean.reshape(tiles, 1, cells),
        state_perturb.reshape(tiles, cells, members),
        held_w,
    )
    return result.reshape(tile_rows, tile_cols, cells, members)


def solution(mesh):
    return jax.shard_map(
        local,
        mesh=mesh,
        in_specs=(
            P(("lon", "lat"), None, None),
            P(("lon", "lat"), None),
            P(),
            P("lon", "lat", None),
            P("lon", "lat", None),
            P("lon", "lat", None),
            P("lon", "lat", None, None),
            P("lon", "lat", None),
            P("lon", "lat", None),
        ),
        out_specs=P("lon", "lat", None, None),
        check_vma=False,
    )
```

```python
import functools

import jax
import jax.numpy as jnp
from jax import lax
from jax.experimental import pallas as pl
from jax.experimental.pallas import tpu as pltpu
from jax.sharding import PartitionSpec as P

ITERS = 5
FAST = 4
TAIL = 16
SIDE = 4
GRANT = 8 << 20
bf16 = jnp.bfloat16
f32 = jnp.float32
highest = lax.Precision.HIGHEST


def product(a, b):
    rest = jnp.dot(a[1].astype(bf16), b[1].astype(bf16), preferred_element_type=f32)
    return a[0] * b[0], a[0] * b[1] + b[0] * a[1] + rest


def step_factor(a):
    return 1.5 - 0.5 * a[0], -0.5 * a[1]


def row_times(vector, a):
    hi = vector.astype(bf16).astype(f32)
    rows = jnp.concatenate([hi, vector - hi, jnp.zeros((14, vector.shape[1]), f32)], axis=0)
    got = jnp.dot(rows.astype(bf16), a[1].astype(bf16), preferred_element_type=f32)
    return a[0] * vector + jnp.sum(got[:2], axis=0, keepdims=True)


def places_of(half):
    row = lax.broadcasted_iota(jnp.int32, (half, half), 0)
    col = lax.broadcasted_iota(jnp.int32, (half, half), 1)
    return row, col


def pack(matrix, vector_rows):
    half = matrix.shape[0] // 2
    row, col = places_of(half)
    lower_right = matrix[half:, half:]
    both = jnp.where(row >= col, matrix[:half, :half], lower_right)
    diagonal = jnp.sum(jnp.where(row == col, lower_right, 0.0), axis=0, keepdims=True)
    hi = diagonal.astype(bf16).astype(f32)
    tail = jnp.concatenate(
        [hi, diagonal - hi, vector_rows, jnp.zeros((TAIL - 6, half), f32)], axis=0
    )
    return matrix[half:, :half], both, tail


def unpack(total):
    half = total.shape[1]
    members = 2 * half
    row, col = places_of(half)
    corner = total[:half]
    both = total[half:members]
    turned = both.T
    diagonal = total[members : members + 1] + total[members + 1 : members + 2]
    upper_left = jnp.where(row >= col, both, turned)
    lower_right = jnp.where(
        row == col, jnp.broadcast_to(diagonal, (half, half)), jnp.where(row < col, both, turned)
    )
    matrix = jnp.concatenate(
        [
            jnp.concatenate([upper_left, corner.T], axis=1),
            jnp.concatenate([corner, lower_right], axis=1),
        ],
        axis=0,
    )
    vector = jnp.concatenate(
        [
            total[members + 2 + h : members + 3 + h] + total[members + 4 + h : members + 5 + h]
            for h in range(2)
        ],
        axis=1,
    )
    return matrix, vector


def vector_rows(vector, half):
    hi = vector.astype(bf16).astype(f32)
    lo = vector - hi
    return jnp.concatenate([hi[:, :half], hi[:, half:], lo[:, :half], lo[:, half:]], axis=0)


def join_kernel(start, *refs):
    pieces, (y_ref, sem) = refs[:-2], refs[-2:]
    copies = []
    at = start
    for i, piece in enumerate(pieces):
        copies.append(
            pltpu.make_async_copy(piece, y_ref.at[pl.ds(at, piece.shape[0])], sem.at[i])
        )
        copies[-1].start()
        at += piece.shape[0]
    for copy in copies:
        copy.wait()


def gram_kernel(points, ranks, call, outs, slots, wts, drive_ref, y_ref, *refs):
    added, outs, acc_ref = refs[: -outs - 1], refs[-outs - 1 : -1], refs[-1]
    half = y_ref.shape[2] // 2
    targets = [(o, way) for o in range(len(outs)) for way in range(outs[o].shape[0])]
    dests = [slots[wts.shape[0] + call, i] for i in range(len(targets))]
    most = jnp.int32(0)
    for (o, way), dest in zip(targets, dests):
        o_ref = outs[o]
        for p in range(points):
            at = p * ranks
            ys = [y_ref[slots[dest, at + k]] for k in range(FAST)]
            yw = [(ys[k].astype(f32) * wts[dest, at + k]).astype(bf16) for k in range(FAST)]
            gram = lax.dot_general(
                jnp.concatenate(yw, axis=0),
                jnp.concatenate(ys, axis=0),
                (((0,), (0,)), ((), ())),
                preferred_element_type=f32,
            )
            for i, part in enumerate(pack(gram, drive_ref[dest, p])):
                at = pl.ds(i * half, part.shape[0])
                if added:
                    part = part + added[o][way, p, at].astype(f32)
                o_ref[way, p, at] = part.astype(bf16)
            most = jnp.maximum(most, slots[dest, points * ranks + p])

    @pl.when(most > FAST)
    def _():
        for (o, way), dest in zip(targets, dests):
            o_ref = outs[o]
            for p in range(points):
                count = slots[dest, points * ranks + p]

                @pl.when(count > FAST)
                def _(o_ref=o_ref, dest=dest, way=way, p=p, count=count):
                    acc_ref[...] = jnp.zeros_like(acc_ref)

                    @pl.loop(FAST, count)
                    def _(k):
                        y = y_ref[slots[dest, p * ranks + k]]
                        w = (y.astype(f32) * wts[dest, p * ranks + k]).astype(bf16)
                        acc_ref[...] += lax.dot_general(
                            w, y, (((0,), (0,)), ((), ())), preferred_element_type=f32
                        )

                    rest = pack(acc_ref[...], jnp.zeros((4, half), f32))
                    for i, part in enumerate(rest):
                        at = pl.ds(i * half, part.shape[0])
                        o_ref[way, p, at] = (o_ref[way, p, at].astype(f32) + part).astype(bf16)


def root_kernel(odd, *refs):
    parts, outs = refs[:-2], refs[-2:]
    points, rows, half = parts[0].shape
    members = 2 * half
    here = range(points)
    eye = (
        lax.broadcasted_iota(jnp.int32, (members, members), 0)
        == lax.broadcasted_iota(jnp.int32, (members, members), 1)
    ).astype(f32)
    scale = 1.0 / (members - 1)
    drives, bounds, uppers, lowers = [], [], [], []
    for p in here:
        total = parts[0][p].astype(f32)
        for part in parts[1:]:
            total = total + part[p].astype(f32)
        cov, drive = unpack(total)
        drives.append(drive * scale)
        system = eye + cov * scale
        bound = jnp.max(
            jnp.sum(jnp.abs(system), axis=0, keepdims=True), axis=1, keepdims=True
        )
        trace = jnp.sum(
            jnp.sum(system * eye, axis=0, keepdims=True), axis=1, keepdims=True
        )
        level = trace * (1.0 / members)
        inverse = 1.0 / bound
        bounds.append(bound)
        uppers.append((level * inverse, (system - level * eye) * inverse))
    lowers = [step_factor(uppers[p]) for p in here]
    uppers = [product(uppers[p], lowers[p]) for p in here]
    for sweep in range(1, ITERS):
        factors = [step_factor(product(lowers[p], uppers[p])) for p in here]
        if sweep < ITERS - 1:
            uppers = [product(uppers[p], factors[p]) for p in here]
        lowers = [product(factors[p], lowers[p]) for p in here]
    for p in here:
        norm = lax.rsqrt(bounds[p])
        root = (lowers[p][0] * norm, lowers[p][1] * norm)
        shift = row_times(row_times(drives[p], root), root)
        corner, both, tail = (
            v.astype(bf16) for v in pack(root[1] + root[0] * eye, vector_rows(shift, half))
        )
        row = p // 2
        for flip in range(2):

            @pl.when(odd[0] == flip)
            def _(o_ref=outs[(p + 1 + flip) % 2], row=row, corner=corner, both=both, tail=tail):
                o_ref[row, :half] = corner
                o_ref[row, half:members] = both
                o_ref[row, members:] = tail


def state_kernel(places, mixing, mean_ref, pert_ref, w_ref, o_ref):
    step = pl.program_id(0)
    count, cells, members = o_ref.shape
    ones = jnp.ones((TAIL, members), bf16)
    for t in range(count):
        tile = step * count + t
        total = mixing[tile, 0] * w_ref[places[tile, 0]].astype(f32)
        for j in range(1, 4):
            total = total + mixing[tile, j] * w_ref[places[tile, j]].astype(f32)
        root, shift = unpack(total)
        turned = (root + shift).astype(bf16)
        mean = mean_ref[t]
        hi = mean.astype(bf16).astype(f32)
        mid = (mean - hi).astype(bf16).astype(f32)
        thirds = jnp.concatenate(
            [hi, mid, mean - hi - mid, jnp.zeros((TAIL - 3, cells), f32)], axis=0
        ).astype(bf16)
        moved = lax.dot_general(
            pert_ref[t], turned, (((1,), (1,)), ((), ())), preferred_element_type=f32
        )
        mean = lax.dot_general(
            thirds, ones, (((0,), (0,)), ((), ())), preferred_element_type=f32
        )
        o_ref[t] = (mean + moved).astype(bf16)


def column_of(rows):
    size = lax.axis_size("lon")
    up = [(i, (i + 2) % size) for i in range(size)]
    down = [(i, (i - 2) % size) for i in range(size)]
    cut = rows.shape[0] // 2

    def send(x, pairs):
        return lax.ppermute(x, "lon", pairs)

    def swap(x):
        return lax.ppermute(x, "lon", [(i, i ^ 1) for i in range(size)])

    below = send(rows, up)
    above = send(rows, down)
    far_a = send(below[:cut], up)
    far_b = send(above[cut:], down)
    near = [rows, below, above]
    far = [far_a, far_b]
    return near + [swap(x) for x in near] + far + [swap(x) for x in far]


def place_of(apart, other):
    near = jnp.where(apart == 0, 0, jnp.where(apart == 1, 2, 1)) + 3 * other
    return jnp.where(apart == 2, 6 + other, near)


def turn(stage, k, chips):
    pairs = []
    for lon in range(2 * chips):
        for x in range(SIDE):
            for y in range(SIDE):
                if (lon + stage) % 2 == 0:
                    to = x * SIDE + (y + k) % SIDE
                else:
                    to = (x + k) % SIDE * SIDE + y
                start = lon * SIDE * SIDE
                pairs.append((start + x * SIDE + y, start + to))
    return pairs


def local(
    obs_rows,
    innovations,
    obs_home,
    obs_lists,
    loc_weights,
    state_mean,
    state_perturb,
    interp_ids,
    interp_wts,
):
    lon_count = lax.axis_size("lon")
    lat_count = lax.axis_size("lat")
    lon = lax.axis_index("lon")
    lat = lax.axis_index("lat")
    held, obs_count, members = obs_rows.shape
    half = members // 2
    point_rows, point_cols, list_len = obs_lists.shape
    points = point_rows * point_cols
    ranks = 2 * lon_count
    column_blocks = lon_count * held

    pieces = column_of(obs_rows)
    innovations, _, _ = lax.optimization_barrier((innovations, pieces[1], pieces[2]))
    project = jnp.einsum("lok,lo->lk", obs_rows, innovations, preferred_element_type=f32)
    column_proj = lax.all_to_all(
        jnp.broadcast_to(project, (lon_count, held, members)), "lon", 0, 0, tiled=True
    ).reshape(column_blocks, members)

    ids = obs_lists.reshape(points, list_len)
    live = ids >= 0
    home = jnp.take(obs_home, jnp.maximum(ids, 0))
    column = jnp.where(live, home // held % lat_count, lat_count)
    slot = home // (held * lat_count) * held + home % held
    mask = column[None] == jnp.arange(lat_count, dtype=jnp.int32)[:, None, None]
    rank = jnp.cumsum(mask.astype(jnp.int32), axis=2) - 1
    chosen = mask[..., None] & (rank[..., None] == jnp.arange(ranks, dtype=jnp.int32))
    slots_f = jnp.sum(jnp.where(chosen, slot.astype(f32)[None, :, :, None], 0.0), axis=2)
    wts_f = jnp.sum(
        jnp.where(chosen, loc_weights.reshape(1, points, list_len, 1), 0.0), axis=2
    )
    counts = jnp.sum(mask.astype(f32), axis=2)
    asked = jnp.concatenate(
        [
            slots_f.reshape(lat_count, points * ranks),
            counts,
            wts_f.reshape(lat_count, points * ranks),
        ],
        axis=1,
    )
    asked = lax.all_to_all(asked, "lat", 0, 0, tiled=True)
    cut = points * ranks + points
    wts = asked[:, cut:]
    named = asked[:, : points * ranks].astype(jnp.int32)
    from_lon = named // held
    apart = (from_lon // 2 - lon // 2) % (lon_count // 2)
    other = (from_lon + lon) % 2
    slots = jnp.concatenate(
        [
            place_of(apart, other) * held + named % held,
            asked[:, points * ranks : cut].astype(jnp.int32),
        ],
        axis=1,
    )

    spread = jnp.sum(
        jnp.where(
            named.reshape(lat_count * points, ranks, 1)
            == jnp.arange(column_blocks, dtype=jnp.int32),
            wts.reshape(lat_count * points, ranks, 1),
            0.0,
        ),
        axis=1,
    )
    drive = jnp.dot(spread, column_proj, precision=highest)
    drive_hi = drive.astype(bf16).astype(f32)
    drive_rows = jnp.concatenate(
        [v.reshape(lat_count, points, 2, half) for v in (drive_hi, drive - drive_hi)], axis=2
    )

    smem = pl.BlockSpec(memory_space=pltpu.SMEM)
    vmem = pl.BlockSpec(memory_space=pltpu.VMEM)
    rows = members + TAIL
    x, y = lat // SIDE, lat % SIDE
    y_first = lon % 2 == 0

    early, late = (0, 1), (2, 3)
    calls = (
        ((2, early), (2, late)),
        ((1, late), (3, early)),
        ((1, early), (3, late)),
        ((0, early + late),),
    )
    orders = []
    for results in calls:
        first = jnp.asarray([k for k, ways in results for _ in ways], jnp.int32)
        then = jnp.asarray([way for _, ways in results for way in ways], jnp.int32)
        along_x, along_y = jnp.where(y_first, then, first), jnp.where(y_first, first, then)
        orders.append((x + along_x) % SIDE * SIDE + (y + along_y) % SIDE)
    orders = jnp.pad(jnp.stack(orders), ((0, 0), (0, slots.shape[1] - SIDE)))
    slots = jnp.concatenate([slots, orders], axis=0)

    def gram(call, *added):
        results = calls[call]
        return pl.pallas_call(
            functools.partial(gram_kernel, points, ranks, call, len(results)),
            out_shape=[
                jax.ShapeDtypeStruct((len(ways), points, rows, half), bf16)
                for _, ways in results
            ],
            in_specs=[smem, smem, vmem, vmem] + [vmem] * len(added),
            out_specs=[vmem] * len(results),
            scratch_shapes=[pltpu.VMEM((members, members), f32)],
            compiler_params=pltpu.CompilerParams(vmem_limit_bytes=GRANT),
            cost_estimate=pl.CostEstimate(
                flops=2 * 16 * 512 * 256 * 256, bytes_accessed=4 << 20, transcendentals=0
            ),
            name="gram",
        )(slots, wts, drive_rows, column_rows, *added)

    chips = lon_count // 2
    column_rows = pl.pallas_call(
        functools.partial(join_kernel, 0),
        out_shape=jax.ShapeDtypeStruct((column_blocks, obs_count, members), bf16),
        in_specs=[pl.BlockSpec(memory_space=pl.ANY)] * len(pieces),
        out_specs=pl.BlockSpec(memory_space=pl.ANY),
        scratch_shapes=[pltpu.SemaphoreType.DMA((len(pieces),))],
        compiler_params=pltpu.CompilerParams(vmem_limit_bytes=1 << 20),
        name="join",
    )(*pieces)
    axes = ("lon", "lat")
    def send(block, k):
        return lax.ppermute(block, axes, turn(0, k, chips))

    def both_ways(results):
        return [send(results[0], 1), send(results[1], 3)]

    onward = both_ways(gram(0))
    straight = both_ways(gram(1))
    relayed = both_ways(gram(2, *onward))
    (mine,) = gram(3)

    def total(k):
        arrived = (relayed[0], straight[1]) if k in early else (straight[0], relayed[1])
        sums = mine[k].astype(f32)
        for part in arrived:
            sums = sums + part[k % 2].astype(f32)
        return sums

    own = total(0)
    seconds = [
        lax.ppermute(total(k).astype(bf16), axes, turn(1, k, chips)) for k in (2, 1, 3)
    ]

    col = jax.ShapeDtypeStruct((point_rows, rows, half), bf16)
    whole = pl.BlockSpec((points, rows, half), lambda i: (0, 0, 0))
    odd = lat % 2 == 1
    near_col, other_col = pl.pallas_call(
        root_kernel,
        grid=(1,),
        out_shape=(col, col),
        in_specs=[smem] + [whole] * (1 + len(seconds)),
        out_specs=(pl.BlockSpec((point_rows, rows, half), lambda i: (0, 0, 0)),) * 2,
        compiler_params=pltpu.CompilerParams(vmem_limit_bytes=16 << 20),
        cost_estimate=pl.CostEstimate(
            flops=4 * 12 * 2 * 256**3, bytes_accessed=2 << 20, transcendentals=0
        ),
        name="root",
    )((lat % 2).astype(jnp.int32).reshape(1), own, *seconds)

    near_got = lax.ppermute(near_col, "lat", [(i, i ^ 1) for i in range(lat_count)])
    other_got = lax.ppermute(
        other_col, "lat", [(i, (i - 1 ^ 1) + 1) for i in range(1, lat_count - 1)]
    )
    cols = [other_got, other_col, near_col, near_got]
    top = jnp.stack([c[0] for c in cols])
    bottom = jnp.stack([c[1] for c in cols])
    outside = lax.ppermute(
        jnp.where(y_first, top, bottom),
        "lon",
        [(i, (i ^ 1) + (2 if i % 2 else -2)) for i in range(1, lon_count - 1)],
    )
    inside = lax.ppermute(
        jnp.where(y_first, bottom, top), "lon", [(i, i ^ 1) for i in range(lon_count)]
    )
    held_w = jnp.concatenate([top, bottom, outside, inside], axis=0)

    grid_cols = point_cols * lat_count
    tile_rows, tile_cols, cells = state_mean.shape
    tiles = tile_rows * tile_cols
    target_ids = interp_ids.reshape(tiles, 4)
    local_row = target_ids // grid_cols - lon * point_rows
    local_col = target_ids % grid_cols - lat * point_cols + 1
    block = jnp.where(
        local_row < 0,
        jnp.where(y_first, 2, 3),
        jnp.where(local_row >= point_rows, jnp.where(y_first, 3, 2), local_row),
    )
    places = block * 4 + jnp.where(odd, 3 - local_col, local_col)
    per = 4
    result = pl.pallas_call(
        state_kernel,
        grid=(tiles // per,),
        out_shape=jax.ShapeDtypeStruct((tiles, cells, members), bf16),
        in_specs=[
            smem,
            smem,
            pl.BlockSpec((per, 1, cells), lambda i: (i, 0, 0)),
            pl.BlockSpec((per, cells, members), lambda i: (i, 0, 0)),
            vmem,
        ],
        out_specs=pl.BlockSpec((per, cells, members), lambda i: (i, 0, 0)),
        compiler_params=pltpu.CompilerParams(vmem_limit_bytes=12 << 20),
        cost_estimate=pl.CostEstimate(
            flops=2 * 16 * 512 * 256 * 256, bytes_accessed=11 << 20, transcendentals=0
        ),
        name="state",
    )(
        places,
        interp_wts.reshape(tiles, 4),
        state_mean.reshape(tiles, 1, cells),
        state_perturb.reshape(tiles, cells, members),
        held_w,
    )
    return result.reshape(tile_rows, tile_cols, cells, members)


def solution(mesh):
    return jax.shard_map(
        local,
        mesh=mesh,
        in_specs=(
            P(("lon", "lat"), None, None),
            P(("lon", "lat"), None),
            P(),
            P("lon", "lat", None),
            P("lon", "lat", None),
            P("lon", "lat", None),
            P("lon", "lat", None, None),
            P("lon", "lat", None),
            P("lon", "lat", None),
        ),
        out_specs=P("lon", "lat", None, None),
        check_vma=False,
    )
```

```python
import functools

import jax
import jax.numpy as jnp
from jax import lax
from jax.experimental import pallas as pl
from jax.experimental.pallas import tpu as pltpu
from jax.sharding import PartitionSpec as P

ITERS = 5
FAST = 4
TAIL = 16
SIDE = 4
GRANT = 8 << 20
bf16 = jnp.bfloat16
f32 = jnp.float32
highest = lax.Precision.HIGHEST


def product(a, b):
    rest = jnp.dot(a[1].astype(bf16), b[1].astype(bf16), preferred_element_type=f32)
    return a[0] * b[0], a[0] * b[1] + b[0] * a[1] + rest


def step_factor(a):
    return 1.5 - 0.5 * a[0], -0.5 * a[1]


def row_times(vector, a):
    hi = vector.astype(bf16).astype(f32)
    rows = jnp.concatenate([hi, vector - hi, jnp.zeros((14, vector.shape[1]), f32)], axis=0)
    got = jnp.dot(rows.astype(bf16), a[1].astype(bf16), preferred_element_type=f32)
    return a[0] * vector + jnp.sum(got[:2], axis=0, keepdims=True)


def places_of(half):
    row = lax.broadcasted_iota(jnp.int32, (half, half), 0)
    col = lax.broadcasted_iota(jnp.int32, (half, half), 1)
    return row, col


def pack(matrix, vector_rows):
    half = matrix.shape[0] // 2
    row, col = places_of(half)
    lower_right = matrix[half:, half:]
    both = jnp.where(row >= col, matrix[:half, :half], lower_right)
    diagonal = jnp.sum(jnp.where(row == col, lower_right, 0.0), axis=0, keepdims=True)
    hi = diagonal.astype(bf16).astype(f32)
    tail = jnp.concatenate(
        [hi, diagonal - hi, vector_rows, jnp.zeros((TAIL - 6, half), f32)], axis=0
    )
    return matrix[half:, :half], both, tail


def unpack(total):
    half = total.shape[1]
    members = 2 * half
    row, col = places_of(half)
    corner = total[:half]
    both = total[half:members]
    turned = both.T
    diagonal = total[members : members + 1] + total[members + 1 : members + 2]
    upper_left = jnp.where(row >= col, both, turned)
    lower_right = jnp.where(
        row == col, jnp.broadcast_to(diagonal, (half, half)), jnp.where(row < col, both, turned)
    )
    matrix = jnp.concatenate(
        [
            jnp.concatenate([upper_left, corner.T], axis=1),
            jnp.concatenate([corner, lower_right], axis=1),
        ],
        axis=0,
    )
    vector = jnp.concatenate(
        [
            total[members + 2 + h : members + 3 + h] + total[members + 4 + h : members + 5 + h]
            for h in range(2)
        ],
        axis=1,
    )
    return matrix, vector


def vector_rows(vector, half):
    hi = vector.astype(bf16).astype(f32)
    lo = vector - hi
    return jnp.concatenate([hi[:, :half], hi[:, half:], lo[:, :half], lo[:, half:]], axis=0)


def join_kernel(start, *refs):
    pieces, (y_ref, sem) = refs[:-2], refs[-2:]
    copies = []
    at = start
    for i, piece in enumerate(pieces):
        copies.append(
            pltpu.make_async_copy(piece, y_ref.at[pl.ds(at, piece.shape[0])], sem.at[i])
        )
        copies[-1].start()
        at += piece.shape[0]
    for copy in copies:
        copy.wait()


def gram_kernel(points, ranks, call, outs, slots, wts, drive_ref, y_ref, *refs):
    added, outs, acc_ref = refs[: -outs - 1], refs[-outs - 1 : -1], refs[-1]
    half = y_ref.shape[2] // 2
    targets = [(o, way) for o in range(len(outs)) for way in range(outs[o].shape[0])]
    dests = [slots[wts.shape[0] + call, i] for i in range(len(targets))]
    most = jnp.int32(0)
    for (o, way), dest in zip(targets, dests):
        o_ref = outs[o]
        for p in range(points):
            at = p * ranks
            ys = [y_ref[slots[dest, at + k]] for k in range(FAST)]
            yw = [(ys[k].astype(f32) * wts[dest, at + k]).astype(bf16) for k in range(FAST)]
            gram = lax.dot_general(
                jnp.concatenate(yw, axis=0),
                jnp.concatenate(ys, axis=0),
                (((0,), (0,)), ((), ())),
                preferred_element_type=f32,
            )
            for i, part in enumerate(pack(gram, drive_ref[dest, p])):
                at = pl.ds(i * half, part.shape[0])
                if added:
                    part = part + added[o][way, p, at].astype(f32)
                o_ref[way, p, at] = part.astype(bf16)
            most = jnp.maximum(most, slots[dest, points * ranks + p])

    @pl.when(most > FAST)
    def _():
        for (o, way), dest in zip(targets, dests):
            o_ref = outs[o]
            for p in range(points):
                count = slots[dest, points * ranks + p]

                @pl.when(count > FAST)
                def _(o_ref=o_ref, dest=dest, way=way, p=p, count=count):
                    acc_ref[...] = jnp.zeros_like(acc_ref)

                    @pl.loop(FAST, count)
                    def _(k):
                        y = y_ref[slots[dest, p * ranks + k]]
                        w = (y.astype(f32) * wts[dest, p * ranks + k]).astype(bf16)
                        acc_ref[...] += lax.dot_general(
                            w, y, (((0,), (0,)), ((), ())), preferred_element_type=f32
                        )

                    rest = pack(acc_ref[...], jnp.zeros((4, half), f32))
                    for i, part in enumerate(rest):
                        at = pl.ds(i * half, part.shape[0])
                        o_ref[way, p, at] = (o_ref[way, p, at].astype(f32) + part).astype(bf16)


def root_kernel(odd, *refs):
    parts, outs = refs[:-2], refs[-2:]
    points, rows, half = parts[0].shape
    members = 2 * half
    here = range(points)
    eye = (
        lax.broadcasted_iota(jnp.int32, (members, members), 0)
        == lax.broadcasted_iota(jnp.int32, (members, members), 1)
    ).astype(f32)
    scale = 1.0 / (members - 1)
    drives, bounds, uppers, lowers = [], [], [], []
    for p in here:
        at = p // 2 * 2 + (1 - odd[0] if p % 2 == 0 else odd[0])
        total = parts[0][at].astype(f32)
        for part in parts[1:]:
            total = total + part[at].astype(f32)
        cov, drive = unpack(total)
        drives.append(drive * scale)
        system = eye + cov * scale
        bound = jnp.max(
            jnp.sum(jnp.abs(system), axis=0, keepdims=True), axis=1, keepdims=True
        )
        trace = jnp.sum(
            jnp.sum(system * eye, axis=0, keepdims=True), axis=1, keepdims=True
        )
        level = trace * (1.0 / members)
        inverse = 1.0 / bound
        bounds.append(bound)
        uppers.append((level * inverse, (system - level * eye) * inverse))
    lowers = [step_factor(uppers[p]) for p in here]
    uppers = [product(uppers[p], lowers[p]) for p in here]
    for sweep in range(1, ITERS):
        factors = [step_factor(product(lowers[p], uppers[p])) for p in here]
        if sweep < ITERS - 1:
            uppers = [product(uppers[p], factors[p]) for p in here]
        lowers = [product(factors[p], lowers[p]) for p in here]
    for p in here:
        norm = lax.rsqrt(bounds[p])
        root = (lowers[p][0] * norm, lowers[p][1] * norm)
        shift = row_times(row_times(drives[p], root), root)
        corner, both, tail = (
            v.astype(bf16) for v in pack(root[1] + root[0] * eye, vector_rows(shift, half))
        )
        o_ref, row = outs[p % 2], p // 2
        o_ref[row, :half] = corner
        o_ref[row, half:members] = both
        o_ref[row, members:] = tail


def state_kernel(places, mixing, mean_ref, pert_ref, w_ref, o_ref):
    step = pl.program_id(0)
    count, cells, members = o_ref.shape
    ones = jnp.ones((TAIL, members), bf16)
    for t in range(count):
        tile = step * count + t
        total = mixing[tile, 0] * w_ref[places[tile, 0]].astype(f32)
        for j in range(1, 4):
            total = total + mixing[tile, j] * w_ref[places[tile, j]].astype(f32)
        root, shift = unpack(total)
        turned = (root + shift).astype(bf16)
        mean = mean_ref[t]
        hi = mean.astype(bf16).astype(f32)
        mid = (mean - hi).astype(bf16).astype(f32)
        thirds = jnp.concatenate(
            [hi, mid, mean - hi - mid, jnp.zeros((TAIL - 3, cells), f32)], axis=0
        ).astype(bf16)
        moved = lax.dot_general(
            pert_ref[t], turned, (((1,), (1,)), ((), ())), preferred_element_type=f32
        )
        mean = lax.dot_general(
            thirds, ones, (((0,), (0,)), ((), ())), preferred_element_type=f32
        )
        o_ref[t] = (mean + moved).astype(bf16)


def column_of(rows):
    size = lax.axis_size("lon")
    up = [(i, (i + 2) % size) for i in range(size)]
    down = [(i, (i - 2) % size) for i in range(size)]
    cut = rows.shape[0] // 2

    def send(x, pairs):
        return lax.ppermute(x, "lon", pairs)

    def swap(x):
        return lax.ppermute(x, "lon", [(i, i ^ 1) for i in range(size)])

    below = send(rows, up)
    above = send(rows, down)
    far_a = send(below[:cut], up)
    far_b = send(above[cut:], down)
    near = [rows, below, above]
    far = [far_a, far_b]
    return near + [swap(x) for x in near] + far + [swap(x) for x in far]


def place_of(apart, other):
    near = jnp.where(apart == 0, 0, jnp.where(apart == 1, 2, 1)) + 3 * other
    return jnp.where(apart == 2, 6 + other, near)


def turn(stage, k, chips):
    pairs = []
    for lon in range(2 * chips):
        for x in range(SIDE):
            for y in range(SIDE):
                if (lon + stage) % 2 == 0:
                    to = x * SIDE + (y + k) % SIDE
                else:
                    to = (x + k) % SIDE * SIDE + y
                start = lon * SIDE * SIDE
                pairs.append((start + x * SIDE + y, start + to))
    return pairs


def local(
    obs_rows,
    innovations,
    obs_home,
    obs_lists,
    loc_weights,
    state_mean,
    state_perturb,
    interp_ids,
    interp_wts,
):
    lon_count = lax.axis_size("lon")
    lat_count = lax.axis_size("lat")
    lon = lax.axis_index("lon")
    lat = lax.axis_index("lat")
    held, obs_count, members = obs_rows.shape
    half = members // 2
    point_rows, point_cols, list_len = obs_lists.shape
    points = point_rows * point_cols
    ranks = 2 * lon_count
    column_blocks = lon_count * held

    pieces = column_of(obs_rows)
    innovations, _, _ = lax.optimization_barrier((innovations, pieces[1], pieces[2]))
    project = jnp.einsum("lok,lo->lk", obs_rows, innovations, preferred_element_type=f32)
    column_proj = lax.all_to_all(
        jnp.broadcast_to(project, (lon_count, held, members)), "lon", 0, 0, tiled=True
    ).reshape(column_blocks, members)

    ids = obs_lists.reshape(points, list_len)
    live = ids >= 0
    home = jnp.take(obs_home, jnp.maximum(ids, 0))
    column = jnp.where(live, home // held % lat_count, lat_count)
    slot = home // (held * lat_count) * held + home % held
    mask = column[None] == jnp.arange(lat_count, dtype=jnp.int32)[:, None, None]
    rank = jnp.cumsum(mask.astype(jnp.int32), axis=2) - 1
    chosen = mask[..., None] & (rank[..., None] == jnp.arange(ranks, dtype=jnp.int32))
    slots_f = jnp.sum(jnp.where(chosen, slot.astype(f32)[None, :, :, None], 0.0), axis=2)
    wts_f = jnp.sum(
        jnp.where(chosen, loc_weights.reshape(1, points, list_len, 1), 0.0), axis=2
    )
    counts = jnp.sum(mask.astype(f32), axis=2)
    asked = jnp.concatenate(
        [
            slots_f.reshape(lat_count, points * ranks),
            counts,
            wts_f.reshape(lat_count, points * ranks),
        ],
        axis=1,
    )
    asked = lax.all_to_all(asked, "lat", 0, 0, tiled=True)
    cut = points * ranks + points
    wts = asked[:, cut:]
    named = asked[:, : points * ranks].astype(jnp.int32)
    from_lon = named // held
    apart = (from_lon // 2 - lon // 2) % (lon_count // 2)
    other = (from_lon + lon) % 2
    slots = jnp.concatenate(
        [
            place_of(apart, other) * held + named % held,
            asked[:, points * ranks : cut].astype(jnp.int32),
        ],
        axis=1,
    )

    spread = jnp.sum(
        jnp.where(
            named.reshape(lat_count * points, ranks, 1)
            == jnp.arange(column_blocks, dtype=jnp.int32),
            wts.reshape(lat_count * points, ranks, 1),
            0.0,
        ),
        axis=1,
    )
    drive = jnp.dot(spread, column_proj, precision=highest)
    drive_hi = drive.astype(bf16).astype(f32)
    drive_rows = jnp.concatenate(
        [v.reshape(lat_count, points, 2, half) for v in (drive_hi, drive - drive_hi)], axis=2
    )

    smem = pl.BlockSpec(memory_space=pltpu.SMEM)
    vmem = pl.BlockSpec(memory_space=pltpu.VMEM)
    rows = members + TAIL
    x, y = lat // SIDE, lat % SIDE
    y_first = lon % 2 == 0

    early, late = (0, 1), (2, 3)
    calls = (
        ((2, early), (2, late)),
        ((1, late), (3, early)),
        ((1, early), (3, late)),
        ((0, early + late),),
    )
    orders = []
    for results in calls:
        first = jnp.asarray([k for k, ways in results for _ in ways], jnp.int32)
        then = jnp.asarray([way for _, ways in results for way in ways], jnp.int32)
        along_x, along_y = jnp.where(y_first, then, first), jnp.where(y_first, first, then)
        orders.append((x + along_x) % SIDE * SIDE + (y + along_y) % SIDE)
    orders = jnp.pad(jnp.stack(orders), ((0, 0), (0, slots.shape[1] - SIDE)))
    slots = jnp.concatenate([slots, orders], axis=0)

    def gram(call, *added):
        results = calls[call]
        return pl.pallas_call(
            functools.partial(gram_kernel, points, ranks, call, len(results)),
            out_shape=[
                jax.ShapeDtypeStruct((len(ways), points, rows, half), bf16)
                for _, ways in results
            ],
            in_specs=[smem, smem, vmem, vmem] + [vmem] * len(added),
            out_specs=[vmem] * len(results),
            scratch_shapes=[pltpu.VMEM((members, members), f32)],
            compiler_params=pltpu.CompilerParams(vmem_limit_bytes=GRANT),
            cost_estimate=pl.CostEstimate(
                flops=2 * 16 * 512 * 256 * 256, bytes_accessed=4 << 20, transcendentals=0
            ),
            name="gram",
        )(slots, wts, drive_rows, column_rows, *added)

    chips = lon_count // 2
    column_rows = pl.pallas_call(
        functools.partial(join_kernel, 0),
        out_shape=jax.ShapeDtypeStruct((column_blocks, obs_count, members), bf16),
        in_specs=[pl.BlockSpec(memory_space=pl.ANY)] * len(pieces),
        out_specs=pl.BlockSpec(memory_space=pl.ANY),
        scratch_shapes=[pltpu.SemaphoreType.DMA((len(pieces),))],
        compiler_params=pltpu.CompilerParams(vmem_limit_bytes=1 << 20),
        name="join",
    )(*pieces)
    axes = ("lon", "lat")
    def send(block, k):
        return lax.ppermute(block, axes, turn(0, k, chips))

    def both_ways(results):
        return [send(results[0], 1), send(results[1], 3)]

    onward = both_ways(gram(0))
    straight = both_ways(gram(1))
    relayed = both_ways(gram(2, *onward))
    (mine,) = gram(3)

    def total(k):
        arrived = (relayed[0], straight[1]) if k in early else (straight[0], relayed[1])
        sums = mine[k].astype(f32)
        for part in arrived:
            sums = sums + part[k % 2].astype(f32)
        return sums

    own = total(0)
    seconds = [
        lax.ppermute(total(k).astype(bf16), axes, turn(1, k, chips)) for k in (2, 1, 3)
    ]

    col = jax.ShapeDtypeStruct((point_rows, rows, half), bf16)
    whole = pl.BlockSpec((points, rows, half), lambda i: (0, 0, 0))
    odd = lat % 2 == 1
    near_col, other_col = pl.pallas_call(
        root_kernel,
        grid=(1,),
        out_shape=(col, col),
        in_specs=[smem] + [whole] * (1 + len(seconds)),
        out_specs=(pl.BlockSpec((point_rows, rows, half), lambda i: (0, 0, 0)),) * 2,
        compiler_params=pltpu.CompilerParams(vmem_limit_bytes=16 << 20),
        cost_estimate=pl.CostEstimate(
            flops=4 * 12 * 2 * 256**3, bytes_accessed=2 << 20, transcendentals=0
        ),
        name="root",
    )((lat % 2).astype(jnp.int32).reshape(1), own, *seconds)

    near_got = lax.ppermute(near_col, "lat", [(i, i ^ 1) for i in range(lat_count)])
    other_got = lax.ppermute(
        other_col, "lat", [(i, (i - 1 ^ 1) + 1) for i in range(1, lat_count - 1)]
    )
    cols = [other_got, other_col, near_col, near_got]
    top = jnp.stack([c[0] for c in cols])
    bottom = jnp.stack([c[1] for c in cols])
    outside = lax.ppermute(
        jnp.where(y_first, top, bottom),
        "lon",
        [(i, (i ^ 1) + (2 if i % 2 else -2)) for i in range(1, lon_count - 1)],
    )
    inside = lax.ppermute(
        jnp.where(y_first, bottom, top), "lon", [(i, i ^ 1) for i in range(lon_count)]
    )
    held_w = jnp.concatenate([top, bottom, outside, inside], axis=0)

    grid_cols = point_cols * lat_count
    tile_rows, tile_cols, cells = state_mean.shape
    tiles = tile_rows * tile_cols
    target_ids = interp_ids.reshape(tiles, 4)
    local_row = target_ids // grid_cols - lon * point_rows
    local_col = target_ids % grid_cols - lat * point_cols + 1
    block = jnp.where(
        local_row < 0,
        jnp.where(y_first, 2, 3),
        jnp.where(local_row >= point_rows, jnp.where(y_first, 3, 2), local_row),
    )
    places = block * 4 + jnp.where(odd, 3 - local_col, local_col)
    per = 8
    result = pl.pallas_call(
        state_kernel,
        grid=(tiles // per,),
        out_shape=jax.ShapeDtypeStruct((tiles, cells, members), bf16),
        in_specs=[
            smem,
            smem,
            pl.BlockSpec((per, 1, cells), lambda i: (i, 0, 0)),
            pl.BlockSpec((per, cells, members), lambda i: (i, 0, 0)),
            vmem,
        ],
        out_specs=pl.BlockSpec((per, cells, members), lambda i: (i, 0, 0)),
        compiler_params=pltpu.CompilerParams(vmem_limit_bytes=20 << 20),
        cost_estimate=pl.CostEstimate(
            flops=2 * 16 * 512 * 256 * 256, bytes_accessed=11 << 20, transcendentals=0
        ),
        name="state",
    )(
        places,
        interp_wts.reshape(tiles, 4),
        state_mean.reshape(tiles, 1, cells),
        state_perturb.reshape(tiles, cells, members),
        held_w,
    )
    return result.reshape(tile_rows, tile_cols, cells, members)


def solution(mesh):
    return jax.shard_map(
        local,
        mesh=mesh,
        in_specs=(
            P(("lon", "lat"), None, None),
            P(("lon", "lat"), None),
            P(),
            P("lon", "lat", None),
            P("lon", "lat", None),
            P("lon", "lat", None),
            P("lon", "lat", None, None),
            P("lon", "lat", None),
            P("lon", "lat", None),
        ),
        out_specs=P("lon", "lat", None, None),
        check_vma=False,
    )
```
